512 devices in a mesh: blk: 32 (over y_lo, z), rows: 16 (over x, y_hi, core).
Axes of the slice: x: 4, y: 4 (y_hi: 2, y_lo: 2; y = y_hi * 2 + y_lo), z: 16, core: 2. Of those that a mesh axis runs over, the one named last changes fastest.
Arguments:
- snapshots: bfloat16 [4096, 8192], P('blk', 'rows'), may hold values from -6 to 6
- node_owner: int32 [8192, 1], P('rows'), may hold values from 0 to 15; in each aligned block of 512 rows (0 to 511, 512 to 1023, ...) at most 128 rows name the same one
- mass_blocks: bfloat16 [16, 64, 128, 128], P('rows', 'blk'), as said below
- mass_cols: int32 [16, 64], P('rows', 'blk'), may hold values from 0 to 15, as said below
Outputs:
- gram: float32 [4096, 4096], P('rows', 'blk')
The draws below stay inside these ranges and needn't reach their ends.
Inputs may be any that keep to these rules, and one draw needn't show every extreme that they name: `node_owner`: of the nodes of one evolution partition, at most 128 go to one owner, and exactly 128 do for some owner. `mass_cols`: the stored blocks of row block r of an owner have the column blocks r, r - 1 or r, r + 1 or r, and r, in this order; a block whose column is r in any slot but the first is zero. `mass_blocks`: each owner's M_d is symmetric with a positive diagonal that dominates every row.
All inputs are finite; a program needn't handle non-finite values.
Results may differ from the reference program's by a relative error of at most 0.0005.
Values may be sent and summed in bfloat16 or wider, within the bound.
A program may use at most 64 MiB of HBM per device.

```python
import math
import jax
import jax.numpy as jnp
import numpy as np
from jax import lax

NODE_DEV = 512
BS = 128
KB = 4
SNAPS = 4096
NODES = 8192
CAP = 128
SLOTS = 2048
NRB = 16
MB = 64
N_ROWS = 16


def mass_links(key):
    link_key = jax.random.fold_in(key, 11)
    draws = jax.random.randint(link_key, (N_ROWS, NRB), 0, 4)
    inside = jnp.arange(NRB, dtype=jnp.int32)[None, :] < NRB - 1
    upper = jnp.logical_and(draws > 0, inside)
    lower = jnp.concatenate([jnp.zeros((N_ROWS, 1), jnp.bool_), upper[:, :-1]], axis=1)
    return (upper, lower)


def draw_snapshots(key, part):
    key = jax.random.fold_in(key, 31)
    offset = 0.8 * jax.random.normal(jax.random.fold_in(key, 1), (SNAPS, 1), jnp.float32)
    noise = jax.random.normal(jax.random.fold_in(key, 2), (SNAPS, NODES), jnp.float32)
    return jnp.clip(offset + noise, -6.0, 6.0).astype(jnp.bfloat16)


def draw_mass_cols(key, part):
    upper, lower = mass_links(key)
    here = jnp.broadcast_to(jnp.arange(NRB, dtype=jnp.int32)[None, :], (N_ROWS, NRB))
    cols = jnp.stack([here, jnp.where(lower, here - 1, here), jnp.where(upper, here + 1, here), here], axis=-1)
    return cols.reshape(N_ROWS, MB).astype(jnp.int32)


def draw_mass_blocks(key, part):
    upper, lower = mass_links(key)
    bound = 0.3 / BS
    coupling = jax.random.uniform(jax.random.fold_in(key, 21), (N_ROWS, NRB, BS, BS), jnp.float32, 0.0, bound)
    inner = jax.random.uniform(jax.random.fold_in(key, 22), (N_ROWS, NRB, BS, BS), jnp.float32, 0.0, bound)
    top = math.log(3.0)
    diag_vals = jnp.exp(jax.random.uniform(jax.random.fold_in(key, 23), (N_ROWS, NRB, BS), jnp.float32, 0.0, top))
    eye = jnp.eye(BS, dtype=jnp.float32)
    sym = 0.5 * (inner + jnp.swapaxes(inner, -1, -2))
    diag_block = sym * (1.0 - eye) + diag_vals[..., None] * eye
    up_block = coupling * upper[..., None, None].astype(jnp.float32)
    shifted = jnp.concatenate([jnp.zeros((N_ROWS, 1, BS, BS), jnp.float32), coupling[:, :-1]], axis=1)
    low_block = jnp.swapaxes(shifted, -1, -2) * lower[..., None, None].astype(jnp.float32)
    pad_block = jnp.zeros((N_ROWS, NRB, BS, BS), jnp.float32)
    blocks = jnp.stack([diag_block, low_block, up_block, pad_block], axis=2)
    scale = 1.0 / math.sqrt(NODES)
    return (blocks * scale).reshape(N_ROWS, MB, BS, BS).astype(jnp.bfloat16)


def assign_block(rng, own, number, rows, amount, top, most, slope):
    sequence = jax.random.permutation(rng, amount)
    packed, ordinary = shares(amount, rows * top, most, slope, True), shares(amount, rows * top, most, slope, False)
    places = jnp.arange(amount)

    def named(tallies, rotation):
        used = int((tallies > 0).sum())
        fixed = max(1, used // 4)
        moved = fixed + (places - fixed + rotation * (used - fixed)) % max(1, amount - fixed)
        return jnp.zeros((amount,), jnp.int32).at[sequence[jnp.where(places < fixed, places, moved)]].set(jnp.asarray(tallies, jnp.int32))

    tallies = jnp.where(number % 4 == 0, named(packed, number // 4), named(ordinary, number - number // 4 - 1))
    mixed = jax.random.permutation(jax.random.fold_in(own, 3), amount)
    source_of, receiver = mixed[0:amount // 2 * 2:2], mixed[1:amount // 2 * 2:2]
    margin = jnp.minimum(tallies[source_of] - 1, most - tallies[receiver]) // 2
    margin = jnp.where((source_of == sequence[0]) | (receiver == sequence[0]) | (tallies[receiver] == 0), 0, jnp.maximum(margin, 0))
    moved = jax.random.randint(jax.random.fold_in(own, 4), (amount // 2,), 0, 1 << 20) % (margin + 1)
    tallies = tallies.at[source_of].add(-moved).at[receiver].add(moved)
    members = jnp.searchsorted(jnp.cumsum(tallies), jnp.arange(rows * top), side="right").astype(jnp.int32)
    listing = members.reshape(top, rows).T
    listing = listing[jax.random.permutation(jax.random.fold_in(own, 1), rows)]
    rotation = jax.random.randint(jax.random.fold_in(own, 2), (rows, 1), 0, top)
    return jnp.take_along_axis(listing, (jnp.arange(top)[None, :] + rotation) % top, axis=1)


def shares(amount, total, reach, lean, full):
    loads = [(1 << 20) // math.isqrt(grade ** lean) + 1 for grade in range(1, amount + 1)]
    largest = reach if full else min(reach, max(-(-total // amount), total * loads[0] // sum(loads)))
    least = 1 if total - largest >= amount - 1 else 0
    given, spare = [largest] + [least] * (amount - 1), total - largest - least * (amount - 1)
    while spare > 0:
        candidates = [i for i in range(1, amount) if given[i] < largest] or [i for i in range(1, amount) if given[i] < reach]
        whole, budget = sum([loads[i] for i in candidates]), spare
        for i in candidates:
            more = min(reach - given[i], max(1, budget * loads[i] // whole), spare)
            given[i] = given[i] + more
            spare = spare - more
    return np.array(given)


def setup_inputs(seed: int = 0) -> dict:
    seeds = jax.random.split(jax.random.key(seed), 5)
    snapshots = draw_snapshots(jax.random.fold_in(seeds[4], 71), 0)
    node_owner_keys = jax.random.split(jax.random.fold_in(seeds[1], 1), NODES // NODE_DEV)
    node_owner_turns = jax.random.permutation(jax.random.fold_in(seeds[1], 3), NODES // NODE_DEV)
    node_owner = jax.vmap(lambda own, number: assign_block(jax.random.fold_in(seeds[1], 2), own, number, NODE_DEV, N_ROWS, 1, CAP, 2))(node_owner_keys, node_owner_turns).reshape((NODES, 1))
    mass_blocks = draw_mass_blocks(jax.random.fold_in(seeds[4], 71), 0)
    mass_cols = draw_mass_cols(jax.random.fold_in(seeds[4], 71), 0)
    return {"snapshots": snapshots, "node_owner": node_owner, "mass_blocks": mass_blocks, "mass_cols": mass_cols}


def owner_slabs(snapshots, node_owner):
    dest = node_owner[:, 0].reshape(N_ROWS, NODE_DEV)
    owners = jnp.arange(N_ROWS, dtype=jnp.int32)
    onehot = (dest[:, :, None] == owners[None, None, :]).astype(jnp.int32)
    before = (jnp.cumsum(onehot, axis=1) - onehot).astype(jnp.int32)
    rank = jnp.sum(before * onehot, axis=2).astype(jnp.int32)
    target = (dest * SLOTS + owners[:, None] * CAP + rank).astype(jnp.int32)
    slabs = jnp.zeros((SNAPS, N_ROWS * SLOTS), jnp.bfloat16)
    slabs = slabs.at[:, target.reshape(-1)].set(snapshots)
    return slabs.reshape(SNAPS, N_ROWS, SLOTS).transpose(1, 0, 2)


def reference(snapshots, node_owner, mass_blocks, mass_cols):
    slabs = owner_slabs(snapshots, node_owner)
    row_block = (jnp.arange(MB, dtype=jnp.int32) // KB).astype(jnp.int32)
    block_ids = jnp.arange(NRB, dtype=jnp.int32)

    def one_owner(total, inputs):
        slab, blocks, cols = inputs
        split_rows = slab.reshape(SNAPS, NRB, BS)
        picked = split_rows[:, row_block, :].astype(jnp.float32)
        product = jnp.einsum("smi,mij->smj", picked, blocks.astype(jnp.float32))
        placed = (cols[:, None] == block_ids[None, :]).astype(jnp.float32)
        mapped = jnp.einsum("smj,mn->snj", product, placed)
        weighted = mapped.reshape(SNAPS, SLOTS).astype(jnp.bfloat16)
        tile = jnp.dot(weighted, slab.T, preferred_element_type=jnp.float32)
        return total + tile, None

    start = jnp.zeros((SNAPS, SNAPS), jnp.float32)
    gram, unused = lax.scan(one_owner, start, (slabs, mass_blocks, mass_cols))
    return gram
```

```python
import jax
import jax.numpy as jnp
from jax import lax
from jax.experimental import pallas as pl
from jax.experimental.pallas import tpu as pltpu
from jax.sharding import PartitionSpec as P

MESH = pl.DeviceIdType.MESH
F32 = jnp.float32
BF16 = jnp.bfloat16
NZ = 16
NR = 16
ND = 512
SD = 128
T0 = (((0,), (0,)), ((), ()))
T1 = (((1,), (1,)), ((), ()))


def codes_of(raw, q):
    v = raw[q, 16:32, :].astype(F32)
    own = jnp.concatenate([v[i : i + 1, :] for i in range(4)], axis=1)
    rank = jnp.concatenate([v[i : i + 1, :] for i in range(4, 8)], axis=1)
    return own, rank


def onehot(row, n):
    ids = lax.broadcasted_iota(jnp.int32, (n, row.shape[1]), 0).astype(F32)
    return jnp.where(ids == row, 1.0, 0.0).astype(BF16)


def kernel(
    snap, owner, mass, out,
    msg, raw, mz, cbuf, halo, sall, acc, wown, wc, gt, yrecv, xsend, xrecv,
    t_send, t_recv, a_send, a_recv, b_send, b_recv, c_send, c_recv,
    h_send, h_recv, r_send, r_recv, l_send, l_recv, s_send, s_recv,
    w_send, w_recv, y_send, y_recv, x_send, x_recv,
):
    blk, s = lax.axis_index("blk"), lax.axis_index("rows")
    yl, z = blk // NZ, lax.rem(blk, NZ)
    x, yh, c = s // 4, lax.rem(s // 2, 2), lax.rem(s, 2)
    sib = s + 1 - 2 * c

    def zmove(k):
        return lax.rem(z + k + NZ, NZ)

    def to(src, dst, ssem, rsem, b, r):
        return pltpu.make_async_remote_copy(
            src_ref=src, dst_ref=dst, send_sem=ssem, recv_sem=rsem, device_id=(b, r), device_id_type=MESH
        )

    def drain(ref, sem):
        pltpu.make_async_copy(ref, ref, sem).wait()

    barrier = pltpu.get_barrier_semaphore()
    plane = yl * NR + s

    def greet(i, carry):
        other = lax.rem(plane + i, 2 * NR)
        pl.semaphore_signal(
            barrier, inc=1, device_id=((other // NR) * NZ + z, lax.rem(other, NR)), device_id_type=MESH
        )
        return carry

    lax.fori_loop(1, 2 * NR, greet, 0)
    for k in (1, -1, 2, -2, 4, -4, 8):
        pl.semaphore_signal(barrier, inc=1, device_id=(yl * NZ + zmove(k), s), device_id_type=MESH)

    own = owner[...].astype(F32)
    mine = onehot(own, NR)
    before = jnp.where(
        lax.broadcasted_iota(jnp.int32, (ND, ND), 0) < lax.broadcasted_iota(jnp.int32, (ND, ND), 1), 1.0, 0.0
    ).astype(BF16)
    counts = jnp.dot(mine, before, preferred_element_type=F32)
    rank = jnp.sum(mine.astype(F32) * counts, axis=0, keepdims=True)
    row = lax.broadcasted_iota(jnp.int32, (16, 128), 0)
    code = jnp.zeros((16, 128), F32)
    for i in range(4):
        code = jnp.where(row == i, own[:, 128 * i : 128 * i + 128], code)
        code = jnp.where(row == i + 4, rank[:, 128 * i : 128 * i + 128], code)
    code = code.astype(BF16)
    for a in range(NR):
        msg[a, 0:16, :] = mass[a]
        msg[a, 16:32, :] = code
    sall[c, z] = snap[...]
    halo[2 + yl] = snap[...]
    raw[s] = msg[s]

    pl.semaphore_wait(barrier, 2 * NR - 1 + 7)

    def scatter(i, carry):
        a = lax.rem(s + i, NR)
        to(msg.at[a], raw.at[s], t_send, t_recv, blk, a).start()
        return carry

    lax.fori_loop(1, NR, scatter, 0)

    def ring(k, h, right):
        slot = zmove(-(k - 1)) if right else zmove(k - 1)
        ref = sall.at[c, slot, pl.ds(64 * h, 64)]
        ss, rs = (r_send, r_recv) if right else (l_send, l_recv)
        return to(ref, ref, ss.at[k - 1, h], rs.at[k - 1, h], yl * NZ + zmove(1 if right else -1), s)

    def arrived(k, h, right):
        slot = zmove(-k) if right else zmove(k)
        ref = sall.at[c, slot, pl.ds(64 * h, 64)]
        rs = r_recv if right else l_recv
        pltpu.make_async_copy(ref, ref, rs.at[k - 1, h]).wait()

    def sibling(slot):
        ref = sall.at[c, slot]
        return to(ref, ref, s_send.at[slot], s_recv.at[slot], blk, sib)

    for h in range(2):
        for right in (True, False):
            ring(1, h, right).start()
    sibling(z).start()

    def halo_copy(dyl, ds):
        return to(
            snap, halo.at[2 - 2 * ds + yl], h_send.at[dyl, ds + 1], h_recv, lax.rem(yl + dyl, 2) * NZ + z, s + ds
        )

    def halo_each(f):
        for ds in (0, -1, 1):
            for dyl in (0, 1):
                if ds == 0 and dyl == 0:
                    continue
                if ds == 0:
                    f(halo_copy(dyl, ds))
                else:
                    pl.when(jnp.logical_and(s + ds >= 0, s + ds < NR))(lambda dyl=dyl, ds=ds: f(halo_copy(dyl, ds)))

    halo_each(lambda copy: copy.start())

    def ring_step(k):
        for h in range(2):
            for right in (True, False):
                if k == 8 and right != (h == 0):
                    continue
                arrived(k, h, right)
                if k < 7 or (k == 7 and right == (h == 0)):
                    ring(k + 1, h, right).start()
        sibling(zmove(-k)).start()
        if k < 8:
            sibling(zmove(k)).start()

    zt = lax.rem(z + 1, NZ)
    r_blk = yl * 8 + z // 2
    odd = lax.rem(z, 2)
    col = jnp.where(odd == 1, r_blk + 1, jnp.where(s >= 8, r_blk - 1, r_blk))
    col = jnp.clip(col, 0, NR - 1)
    drain(raw.at[0:15], t_recv)
    own_c, rank_c = codes_of(raw, col)
    slices = raw[:, 0:16, :].reshape(256, 128)
    picked = jnp.dot(slices, onehot(rank_c, 128), preferred_element_type=F32)
    kept = jnp.zeros((16, ND), F32)
    for d in range(NR):
        kept = jnp.where(own_c == float(d), picked[16 * d : 16 * d + 16, :], kept)
    mz[zt // 4, lax.rem(zt, 4)] = kept.astype(BF16)
    mine_z = mz.at[zt // 4, lax.rem(zt, 4)]
    for k in (4, -4, 8):
        to(mine_z, mine_z, a_send, a_recv, yl * NZ + zmove(k), s).start()
    ring_step(1)
    drain(mz.at[0:3, 0], a_recv)
    four = mz.at[:, lax.rem(zt, 4)]
    for k in (1, -1, 2):
        to(four, four, b_send, b_recv, yl * NZ + zmove(k), s).start()
    ring_step(2)
    drain(mz.at[:, 0:3], b_recv)

    def spread(f_remote, f_local):
        def send(src, kinds, slot, cc, dyl, sem):
            dst = cbuf.at[kinds, slot]
            here = jnp.logical_and(cc == s, dyl == 0)
            pl.when(jnp.logical_not(here))(
                lambda: f_remote(to(src, dst, sem, c_recv, lax.rem(yl + dyl, 2) * NZ + z, cc))
            )
            if f_local is not None:
                pl.when(here)(lambda: f_local(pltpu.make_async_copy(src, dst, c_recv)))

        def low(w, carry):
            for dyl in range(2):
                send(
                    mz.at[w // 2, pl.ds(2 * lax.rem(w, 2), 2)], pl.ds(0, 2), s, yl * 8 + w, dyl, c_send.at[w, dyl]
                )
            return carry

        def high(w, carry):
            cc = yl * 8 + w - 1

            @pl.when(cc >= 0)
            def _():
                for dyl in range(2):
                    send(mz.at[w // 2, 2 * lax.rem(w, 2) + 1], 2, s - 8, cc, dyl, c_send.at[w, dyl])

            return carry

        @pl.when(s < 8)
        def _():
            lax.fori_loop(1, 8, low, 0)
            for dyl in range(2):
                send(mz.at[0, 1], 1, s, yl * 8, dyl, c_send.at[0, dyl])

            @pl.when(yl == 0)
            def _():
                for dyl in range(2):
                    send(mz.at[0, 0], 0, s, 8 + 0 * yl, dyl, c_send.at[8, dyl])

        @pl.when(s >= 8)
        def _():
            lax.fori_loop(0, 8, high, 0)

    spread(lambda copy: copy.start(), lambda copy: copy.start())
    ring_step(3)

    edge = jnp.logical_or(s == 0, s == NR - 1)

    @pl.when(edge)
    def _():
        drain(halo.at[0:3], h_recv)
        drain(cbuf.at[0:2], c_recv)

    @pl.when(jnp.logical_not(edge))
    def _():
        drain(halo.at[0:5], h_recv)
        drain(cbuf, c_recv)

    acc[...] = jnp.zeros_like(acc)
    own_s, _ = codes_of(raw, s)
    hot_s = onehot(own_s, NR)

    def weigh(j):
        @pl.when(jnp.logical_and(s - 1 + j >= 0, s - 1 + j < NR))
        def _():
            own_j, rank_j = codes_of(raw, s - 1 + j)
            same = lax.dot_general(onehot(own_j, NR), hot_s, T0, preferred_element_type=F32)
            wide = lax.dot_general(onehot(rank_j, 128), cbuf[j].reshape(128, ND), T0, preferred_element_type=F32)
            m = (wide * same).astype(BF16)
            acc[...] += jnp.dot(halo[2 * j : 2 * j + 2].reshape(2 * SD, ND), m, preferred_element_type=F32)

    weigh(0)
    ring_step(4)
    weigh(1)
    ring_step(5)
    weigh(2)
    wown[...] = acc[...].reshape(2, SD, ND).astype(BF16)
    wc[c] = wown[c]
    w_copy = to(wown.at[1 - c], wc.at[c], w_send, w_recv, blk, sib)
    w_copy.start()
    ring_step(6)
    drain(wc.at[0], w_recv)

    def piece(zz, f):
        home = x * 4 + lax.rem(zz // 4, 2) * 2 + lax.rem(zz // 2, 2)
        dst = yrecv.at[yl, yh, zz // 8, lax.rem(zz, 2)]
        far = jnp.logical_or(home != s, c != yl)
        pl.when(far)(lambda: f(to(gt.at[zz], dst, y_send.at[zz], y_recv, c * NZ + z, home)))
        return jnp.logical_not(far), dst

    def tile(zz):
        drain(sall.at[1 - c, zz], s_recv.at[zz])
        g = lax.dot_general(sall[0, zz], wc[0], T1, preferred_element_type=F32)
        gt[zz] = g + lax.dot_general(sall[1, zz], wc[1], T1, preferred_element_type=F32)
        near, dst = piece(zz, lambda copy: copy.start())
        pl.when(near)(lambda: pltpu.make_async_copy(gt.at[zz], dst, y_recv).start())

    tile(z)
    for k in range(1, 7):
        tile(zmove(-k))
        tile(zmove(k))
    ring_step(7)
    tile(zmove(-7))
    tile(zmove(7))
    ring_step(8)
    tile(zmove(8))

    drain(yrecv, y_recv)
    for i in range(4):
        xsend[i] = (yrecv[i // 2, 0, i % 2] + yrecv[i // 2, 1, i % 2]).reshape(256, 128)
        pl.when(x != i)(
            lambda i=i: to(xsend.at[i], xrecv.at[x], x_send.at[i], x_recv, blk, 4 * i + 2 * yh + c).start()
        )
    xrecv[x] = xsend[x]
    drain(xrecv.at[0:3], x_recv)
    out[...] = (xrecv[0] + xrecv[1]) + (xrecv[2] + xrecv[3])

    drain(msg.at[0:15], t_send)
    drain(mz.at[0:3, 0], a_send)
    drain(mz.at[:, 0:3], b_send)
    spread(lambda copy: copy.wait_send(), None)
    halo_each(lambda copy: copy.wait_send())
    for k in range(1, 9):
        for h in range(2):
            for right in (True, False):
                if k < 8 or right == (h == 0):
                    ring(k, h, right).wait_send()

    def left(i, carry):
        sibling(i).wait_send()
        piece(i, lambda copy: copy.wait_send())
        return carry

    lax.fori_loop(0, NZ, left, 0)
    w_copy.wait_send()
    for i in range(4):
        pl.when(x != i)(
            lambda i=i: to(xsend.at[i], xrecv.at[x], x_send.at[i], x_recv, blk, 4 * i + 2 * yh + c).wait_send()
        )


def per_device(snapshots, node_owner, mass_blocks, mass_cols):
    dma = pltpu.SemaphoreType.DMA
    one = dma(())
    vmem = pl.BlockSpec(memory_space=pltpu.VMEM)
    return pl.pallas_call(
        kernel,
        out_shape=jax.ShapeDtypeStruct((256, 128), F32),
        in_specs=[vmem] * 3,
        out_specs=vmem,
        scratch_shapes=[
            pltpu.VMEM((16, 32, 128), BF16),
            pltpu.VMEM((16, 32, 128), BF16),
            pltpu.VMEM((4, 4, 16, ND), BF16),
            pltpu.VMEM((3, 8, 16, ND), BF16),
            pltpu.VMEM((6, SD, ND), BF16),
            pltpu.VMEM((2, NZ, SD, ND), BF16),
            pltpu.VMEM((2 * SD, ND), F32),
            pltpu.VMEM((2, SD, ND), BF16),
            pltpu.VMEM((2, SD, ND), BF16),
            pltpu.VMEM((NZ, 128, 128), F32),
            pltpu.VMEM((2, 2, 2, 2, 128, 128), F32),
            pltpu.VMEM((4, 256, 128), F32),
            pltpu.VMEM((4, 256, 128), F32),
            one, one, one, one, one, one, dma((9, 2)), one,
            dma((2, 3)), one, dma((8, 2)), dma((8, 2)), dma((8, 2)), dma((8, 2)), dma((NZ,)), dma((NZ,)),
            one, one, dma((NZ,)), one, dma((4,)), one,
        ],
        compiler_params=pltpu.CompilerParams(
            collective_id=0, has_side_effects=True, vmem_limit_bytes=48 * 1024 * 1024
        ),
        cost_estimate=pl.CostEstimate(flops=1200000000, bytes_accessed=400000, transcendentals=0),
    )(snapshots, node_owner.reshape(1, ND), mass_blocks.reshape(16, 16, 128))


def solution(mesh):
    placed = (P("blk", "rows"), P("rows", None), P("rows", "blk", None, None), P("rows", "blk"))
    return jax.shard_map(
        per_device, mesh=mesh, in_specs=placed, out_specs=P("rows", "blk"), check_vma=False
    )
```

```python
import jax
import jax.numpy as jnp
from jax import lax
from jax.experimental import pallas as pl
from jax.experimental.pallas import tpu as pltpu
from jax.sharding import PartitionSpec as P

MESH = pl.DeviceIdType.MESH
F32 = jnp.float32
BF16 = jnp.bfloat16
NZ = 16
NR = 16
ND = 512
SD = 128
NCH = 4
CH = SD // NCH
T0 = (((0,), (0,)), ((), ()))
T1 = (((1,), (1,)), ((), ()))


def codes_of(raw, q):
    v = raw[q, 16:32, :].astype(F32)
    own = jnp.concatenate([v[i : i + 1, :] for i in range(4)], axis=1)
    rank = jnp.concatenate([v[i : i + 1, :] for i in range(4, 8)], axis=1)
    return own, rank


def onehot(row, n):
    ids = lax.broadcasted_iota(jnp.int32, (n, row.shape[1]), 0).astype(F32)
    return jnp.where(ids == row, 1.0, 0.0).astype(BF16)


def kernel(
    snap, owner, mass, out,
    own_v, mass_v, msg, raw, mz, cbuf, halo, sall, acc, wown, wc, gt, yrecv, xsend, xrecv,
    i_sem, t_send, t_recv, a_send, a_recv, b_send, b_recv, c_send, c_recv,
    h_send, h_recv, z_send, r_recv, l_recv, s_send, s_recv,
    w_send, w_recv, y_send, y_recv, x_send, x_recv,
):
    blk, s = lax.axis_index("blk"), lax.axis_index("rows")
    yl, z = blk // NZ, lax.rem(blk, NZ)
    x, yh, c = s // 4, lax.rem(s // 2, 2), lax.rem(s, 2)
    sib = s + 1 - 2 * c

    def zmove(k):
        return lax.rem(z + k + NZ, NZ)

    def to(src, dst, ssem, rsem, b, r):
        return pltpu.make_async_remote_copy(
            src_ref=src, dst_ref=dst, send_sem=ssem, recv_sem=rsem, device_id=(b, r), device_id_type=MESH
        )

    def drain(ref, sem):
        pltpu.make_async_copy(ref, ref, sem).wait()

    barrier = pltpu.get_barrier_semaphore()
    for k in (8, 4, -4, 2, -2, 1, -1):
        pl.semaphore_signal(barrier, inc=1, device_id=(yl * NZ + zmove(k), s), device_id_type=MESH)
    plane = yl * NR + s

    def greet(i, carry):
        other = lax.rem(plane + i, 2 * NR)
        pl.semaphore_signal(
            barrier, inc=1, device_id=((other // NR) * NZ + z, lax.rem(other, NR)), device_id_type=MESH
        )
        return carry

    lax.fori_loop(1, 2 * NR, greet, 0)

    in_own = pltpu.make_async_copy(owner, own_v, i_sem.at[0])
    in_mass = pltpu.make_async_copy(mass, mass_v, i_sem.at[1])
    in_snap = pltpu.make_async_copy(snap, sall.at[c, z], i_sem.at[2])
    in_own.start()
    in_mass.start()
    in_snap.start()

    before = jnp.where(
        lax.broadcasted_iota(jnp.int32, (ND, ND), 0) < lax.broadcasted_iota(jnp.int32, (ND, ND), 1), 1.0, 0.0
    ).astype(BF16)
    in_own.wait()
    own = own_v[...].astype(F32)
    mine = onehot(own, NR)
    counts = jnp.dot(mine, before, preferred_element_type=F32)
    rank = jnp.sum(mine.astype(F32) * counts, axis=0, keepdims=True)
    row = lax.broadcasted_iota(jnp.int32, (16, 128), 0)
    code = jnp.zeros((16, 128), F32)
    for i in range(4):
        code = jnp.where(row == i, own[:, 128 * i : 128 * i + 128], code)
        code = jnp.where(row == i + 4, rank[:, 128 * i : 128 * i + 128], code)
    code = code.astype(BF16)
    odd = lax.rem(z, 2)
    in_mass.wait()
    for a in range(NR):
        msg[a, 0:16, :] = mass_v[jnp.where(odd == 1, a // 2, a)]
        msg[a, 16:32, :] = code
    raw[s] = msg[s]
    in_snap.wait()

    pl.semaphore_wait(barrier, 2 * NR - 1 + 7)

    def scatter(i, carry):
        a = lax.rem(s + i, NR)
        to(msg.at[a], raw.at[s], t_send, t_recv, blk, a).start()
        return carry

    lax.fori_loop(1, NR, scatter, 0)

    def ring(k, h, right):
        ref = sall.at[c, zmove(1 - k if right else k - 1), pl.ds(CH * h, CH)]
        rs = r_recv if right else l_recv
        return to(ref, ref, z_send, rs.at[k - 1, h], yl * NZ + zmove(1 if right else -1), s)

    def on_ring(k, h, right):
        return k < 8 or right == (h < NCH // 2)

    def sibling(k):
        for slot in {0: (0,), 8: (8,)}.get(k, (-k, k)):
            ref = sall.at[c, zmove(slot)]
            to(ref, ref, s_send, s_recv.at[max(k - 5, 0)], blk, sib).start()

    def ring_step(k):
        for h in range(NCH):
            for right in (True, False):
                if on_ring(k, h, right):
                    ref = sall.at[c, zmove(-k if right else k), pl.ds(CH * h, CH)]
                    drain(ref, (r_recv if right else l_recv).at[k - 1, h])
                    if k < 8 and on_ring(k + 1, h, right):
                        ring(k + 1, h, right).start()
        sibling(k)

    for h in range(NCH):
        for right in (True, False):
            ring(1, h, right).start()
    sibling(0)

    def halo_copy(dyl, ds):
        return to(
            sall.at[c, z], halo.at[2 - 2 * ds + yl], h_send, h_recv, lax.rem(yl + dyl, 2) * NZ + z, s + ds
        )

    for ds in (0, -1, 1):
        for dyl in (0, 1):
            if ds == 0:
                if dyl == 1:
                    halo_copy(dyl, ds).start()
            else:
                pl.when(jnp.logical_and(s + ds >= 0, s + ds < NR))(
                    lambda dyl=dyl, ds=ds: halo_copy(dyl, ds).start()
                )
    halo[2 + yl] = sall[c, z]

    useful = jnp.logical_or(odd == 0, lax.rem(s, 2) == 0)
    kind = jnp.where(odd == 1, 0, jnp.where(s < 8, 1, 2))
    part = jnp.where(odd == 1, s // 2, lax.rem(s, 8))
    shift = jnp.where(odd == 1, 1, jnp.where(s < 8, 0, -1))
    col = jnp.clip(yl * 8 + z // 2 + shift, 0, NR - 1)
    drain(raw.at[0:15], t_recv)

    @pl.when(useful)
    def _():
        own_c, rank_c = codes_of(raw, col)
        slices = raw[:, 0:16, :].reshape(256, 128)
        picked = jnp.dot(slices, onehot(rank_c, 128), preferred_element_type=F32)
        kept = jnp.zeros((16, ND), F32)
        for d in range(NR):
            kept = jnp.where(own_c == float(d), picked[16 * d : 16 * d + 16, :], kept)
        mz[z // 4] = kept.astype(BF16)
        for k in (8, 4, -4):
            to(mz.at[z // 4], mz.at[z // 4], a_send, a_recv, yl * NZ + zmove(k), s).start()

    ring_step(1)
    ring_step(2)

    def spread(f_remote, f_local):
        def each(m, carry):
            cc = yl * 8 + (lax.rem(z, 4) + 4 * m) // 2 + shift
            fits = jnp.logical_and(useful, jnp.logical_and(cc >= 0, cc < NR))
            dst = cbuf.at[kind, part]
            for dyl in range(2):
                here = jnp.logical_and(cc == s, dyl == 0)
                pl.when(jnp.logical_and(fits, jnp.logical_not(here)))(
                    lambda dyl=dyl: f_remote(
                        to(mz.at[m], dst, c_send.at[m, dyl], c_recv, lax.rem(yl + dyl, 2) * NZ + z, cc)
                    )
                )
                if f_local is not None and dyl == 0:
                    pl.when(jnp.logical_and(fits, here))(
                        lambda: f_local(pltpu.make_async_copy(mz.at[m], dst, c_recv))
                    )
            return carry

        lax.fori_loop(0, 4, each, 0)

    pl.when(useful)(lambda: drain(mz.at[0:3], a_recv))
    spread(lambda copy: copy.start(), lambda copy: copy.start())
    ring_step(3)
    ring_step(4)

    got = jnp.where(lax.rem(z, 2) == 0, jnp.where(lax.rem(z - 2 * s + 64, 4) == 0, 1, 2), 0)
    has = jnp.logical_and(
        jnp.logical_or(lax.rem(z, 2) == 0, lax.rem(z - 2 * s + 65, 4) == 0),
        jnp.logical_and(jnp.logical_or(got != 0, s > 0), jnp.logical_or(got != 2, s < NR - 1)),
    )
    got = jnp.where(has, got, 3)

    @pl.when(has)
    def _():
        drain(cbuf.at[0], c_recv)
        for k in (2, 1, -1):
            to(cbuf.at[got], cbuf.at[got], b_send, b_recv.at[got], yl * NZ + zmove(k), s).start()

    ring_step(5)

    acc[...] = jnp.zeros_like(acc)
    own_s, _ = codes_of(raw, s)
    hot_s = onehot(own_s, NR)
    edge = jnp.logical_or(s == 0, s == NR - 1)
    pl.when(edge)(lambda: drain(halo.at[0:3], h_recv))
    pl.when(jnp.logical_not(edge))(lambda: drain(halo.at[0:5], h_recv))

    def weigh(j):
        @pl.when(jnp.logical_and(s - 1 + j >= 0, s - 1 + j < NR))
        def _():
            pl.when(got != j)(lambda: drain(cbuf.at[j], b_recv.at[j]))
            own_j, rank_j = codes_of(raw, s - 1 + j)
            same = lax.dot_general(onehot(own_j, NR), hot_s, T0, preferred_element_type=F32)
            wide = lax.dot_general(onehot(rank_j, 128), cbuf[j].reshape(128, ND), T0, preferred_element_type=F32)
            m = (wide * same).astype(BF16)
            acc[...] += jnp.dot(halo[2 * j : 2 * j + 2].reshape(2 * SD, ND), m, preferred_element_type=F32)

    weigh(0)
    weigh(1)
    weigh(2)
    wown[...] = acc[...].reshape(2, SD, ND).astype(BF16)
    to(wown.at[1 - c], wc.at[c], w_send, w_recv, blk, sib).start()
    wc[c] = wown[c]
    ring_step(6)
    drain(wc.at[0], w_recv)

    def tile(slot):
        zz = zmove(slot)
        g = lax.dot_general(sall[0, zz], wc[0], T1, preferred_element_type=F32)
        gt[zz] = g + lax.dot_general(sall[1, zz], wc[1], T1, preferred_element_type=F32)
        late = lax.rem(zz // 2 - z // 2 + 10, 8) // 4
        home = x * 4 + lax.rem(zz // 4, 2) * 2 + lax.rem(zz // 2, 2)
        dst = yrecv.at[yl, yh, zz // 8, lax.rem(zz, 2)]
        far = jnp.logical_or(home != s, c != yl)
        pl.when(far)(lambda: to(gt.at[zz], dst, y_send, y_recv.at[late], c * NZ + z, home).start())
        pl.when(jnp.logical_not(far))(lambda: pltpu.make_async_copy(gt.at[zz], dst, y_recv.at[late]).start())

    drain(sall.at[0, 0:11], s_recv.at[0])
    for k in range(6):
        for slot in (0,) if k == 0 else (-k, k):
            tile(slot)
    drain(sall.at[0, 0:2], s_recv.at[1])
    tile(-6)
    tile(6)
    ring_step(7)
    drain(sall.at[0, 0:2], s_recv.at[2])
    tile(-7)
    tile(7)
    ring_step(8)
    drain(sall.at[0, 0:1], s_recv.at[3])
    tile(8)

    first = 2 * yh + c
    first = jnp.where(lax.rem(first - z // 2 + 10, 8) < 4, 0, 1)
    for late in range(2):
        i = lax.rem(first + late, 2)
        drain(yrecv.at[0:1], y_recv.at[late])
        for y in range(2):
            dest = 2 * y + i
            xsend[dest] = (yrecv[y, 0, i] + yrecv[y, 1, i]).reshape(256, 128)
            pl.when(x != dest)(
                lambda dest=dest: to(
                    xsend.at[dest], xrecv.at[x], x_send, x_recv, blk, 4 * dest + 2 * yh + c
                ).start()
            )
    xrecv[x] = xsend[x]
    drain(xrecv.at[0:3], x_recv)
    out[...] = (xrecv[0] + xrecv[1]) + (xrecv[2] + xrecv[3])

    drain(msg.at[0:15], t_send)
    pl.when(useful)(lambda: drain(mz.at[0:3], a_send))
    spread(lambda copy: copy.wait_send(), None)
    pl.when(has)(lambda: drain(cbuf, b_send))
    pl.when(edge)(lambda: drain(halo.at[0:3], h_send))
    pl.when(jnp.logical_not(edge))(lambda: drain(halo.at[0:5], h_send))
    drain(sall.at[0, 0:15], z_send)
    drain(sall.at[0], s_send)
    drain(wc.at[0], w_send)
    pl.when(c == yl)(lambda: drain(gt.at[0:12], y_send))
    pl.when(c != yl)(lambda: drain(gt, y_send))
    drain(xsend.at[0:3], x_send)


def per_device(snapshots, node_owner, mass_blocks, mass_cols):
    dma = pltpu.SemaphoreType.DMA
    one = dma(())
    return pl.pallas_call(
        kernel,
        out_shape=jax.ShapeDtypeStruct((256, 128), F32),
        in_specs=[pl.BlockSpec(memory_space=pl.ANY)] * 3,
        out_specs=pl.BlockSpec(memory_space=pltpu.VMEM),
        scratch_shapes=[
            pltpu.VMEM((1, ND), jnp.int32),
            pltpu.VMEM((16, 16, 128), BF16),
            pltpu.VMEM((16, 32, 128), BF16),
            pltpu.VMEM((16, 32, 128), BF16),
            pltpu.VMEM((4, 16, ND), BF16),
            pltpu.VMEM((3, 8, 16, ND), BF16),
            pltpu.VMEM((6, SD, ND), BF16),
            pltpu.VMEM((2, NZ, SD, ND), BF16),
            pltpu.VMEM((2 * SD, ND), F32),
            pltpu.VMEM((2, SD, ND), BF16),
            pltpu.VMEM((2, SD, ND), BF16),
            pltpu.VMEM((NZ, 128, 128), F32),
            pltpu.VMEM((2, 2, 2, 2, 128, 128), F32),
            pltpu.VMEM((4, 256, 128), F32),
            pltpu.VMEM((4, 256, 128), F32),
            dma((3,)), one, one, one, one, one, dma((3,)), dma((4, 2)), one,
            one, one, one, dma((8, NCH)), dma((8, NCH)), one, dma((4,)),
            one, one, one, dma((2,)), one, one,
        ],
        compiler_params=pltpu.CompilerParams(
            collective_id=0, has_side_effects=True, vmem_limit_bytes=64 * 1024 * 1024 - 64 * 1024
        ),
        cost_estimate=pl.CostEstimate(flops=1200000000, bytes_accessed=400000, transcendentals=0),
    )(snapshots, node_owner.reshape(1, ND), mass_blocks.reshape(16, 16, 128))


def solution(mesh):
    placed = (P("blk", "rows"), P("rows", None), P("rows", "blk", None, None), P("rows", "blk"))
    return jax.shard_map(
        per_device, mesh=mesh, in_specs=placed, out_specs=P("rows", "blk"), check_vma=False
    )
```

```python
import jax
import jax.numpy as jnp
from jax import lax
from jax.experimental import pallas as pl
from jax.experimental.pallas import tpu as pltpu
from jax.sharding import PartitionSpec as P

MESH = pl.DeviceIdType.MESH
F32 = jnp.float32
BF16 = jnp.bfloat16
NZ = 16
NR = 16
ND = 512
SD = 128
NCH = 4
CH = SD // NCH
FULL = 32767.0
T0 = (((0,), (0,)), ((), ()))
T1 = (((1,), (1,)), ((), ()))


def codes_of(raw, q):
    v = raw[q, 16:32, :].astype(F32)
    own = jnp.concatenate([v[i : i + 1, :] for i in range(4)], axis=1)
    rank = jnp.concatenate([v[i : i + 1, :] for i in range(4, 8)], axis=1)
    return own, rank


def onehot(row, n):
    ids = lax.broadcasted_iota(jnp.int32, (n, row.shape[1]), 0).astype(F32)
    return jnp.where(ids == row, 1.0, 0.0).astype(BF16)


def encode(g, ref, *at):
    top = jnp.clip(jnp.max(jnp.abs(g), axis=0, keepdims=True), 1e-30, 1e30)
    e = jnp.ceil(jnp.log2(top))
    q = jnp.round(g * (FULL * jnp.exp2(-e)))
    ref[(*at, slice(0, 256), slice(None))] = q.astype(jnp.int32).astype(jnp.int16)
    ref[(*at, slice(256, 272), slice(None))] = jnp.broadcast_to(e, (16, 128)).astype(jnp.int32).astype(jnp.int16)


def decode(v):
    e = v[256:272, :].astype(jnp.int32).astype(F32)[0:1, :]
    return v[0:256, :].astype(jnp.int32).astype(F32) * (jnp.exp2(e) * (1.0 / FULL))


def kernel(
    snap, owner, mass, out,
    own_v, mass_v, msg, raw, mz, cbuf, halo, sall, acc, wown, wc, gt, yrecv, xsend, xrecv, xown,
    i_sem, t_send, t_recv, a_send, a_recv, b_send, b_recv, c_send, c_recv,
    h_send, h_recv, z_send, r_recv, l_recv, s_send, s_recv,
    w_send, w_recv, y_send, y_recv, x_send, x_recv,
):
    blk, s = lax.axis_index("blk"), lax.axis_index("rows")
    yl, z = blk // NZ, lax.rem(blk, NZ)
    x, yh, c = s // 4, lax.rem(s // 2, 2), lax.rem(s, 2)
    sib = s + 1 - 2 * c

    def zmove(k):
        return lax.rem(z + k + NZ, NZ)

    def to(src, dst, ssem, rsem, b, r):
        return pltpu.make_async_remote_copy(
            src_ref=src, dst_ref=dst, send_sem=ssem, recv_sem=rsem, device_id=(b, r), device_id_type=MESH
        )

    def drain(ref, sem):
        pltpu.make_async_copy(ref, ref, sem).wait()

    barrier = pltpu.get_barrier_semaphore()
    for k in (8, 4, -4, 2, -2, 1, -1):
        pl.semaphore_signal(barrier, inc=1, device_id=(yl * NZ + zmove(k), s), device_id_type=MESH)
    plane = yl * NR + s

    def greet(i, carry):
        other = lax.rem(plane + i, 2 * NR)
        pl.semaphore_signal(
            barrier, inc=1, device_id=((other // NR) * NZ + z, lax.rem(other, NR)), device_id_type=MESH
        )
        return carry

    lax.fori_loop(1, 2 * NR, greet, 0)

    in_own = pltpu.make_async_copy(owner, own_v, i_sem.at[0])
    in_mass = pltpu.make_async_copy(mass, mass_v, i_sem.at[1])
    in_snap = pltpu.make_async_copy(snap, sall.at[c, z], i_sem.at[2])
    in_own.start()
    in_mass.start()
    in_snap.start()

    before = jnp.where(
        lax.broadcasted_iota(jnp.int32, (ND, ND), 0) < lax.broadcasted_iota(jnp.int32, (ND, ND), 1), 1.0, 0.0
    ).astype(BF16)
    in_own.wait()
    own = own_v[...].astype(F32)
    mine = onehot(own, NR)
    counts = jnp.dot(mine, before, preferred_element_type=F32)
    rank = jnp.sum(mine.astype(F32) * counts, axis=0, keepdims=True)
    row = lax.broadcasted_iota(jnp.int32, (16, 128), 0)
    code = jnp.zeros((16, 128), F32)
    for i in range(4):
        code = jnp.where(row == i, own[:, 128 * i : 128 * i + 128], code)
        code = jnp.where(row == i + 4, rank[:, 128 * i : 128 * i + 128], code)
    code = code.astype(BF16)
    odd = lax.rem(z, 2)
    in_mass.wait()
    for a in range(NR):
        msg[a, 0:16, :] = mass_v[jnp.where(odd == 1, a // 2, a)]
        msg[a, 16:32, :] = code
    raw[s] = msg[s]
    in_snap.wait()

    pl.semaphore_wait(barrier, 2 * NR - 1 + 7)

    def scatter(i, carry):
        a = lax.rem(s + i, NR)
        to(msg.at[a], raw.at[s], t_send, t_recv, blk, a).start()
        return carry

    lax.fori_loop(1, NR, scatter, 0)

    def ring(k, h, right):
        ref = sall.at[c, zmove(1 - k if right else k - 1), pl.ds(CH * h, CH)]
        rs = r_recv if right else l_recv
        return to(ref, ref, z_send, rs.at[k - 1, h], yl * NZ + zmove(1 if right else -1), s)

    def on_ring(k, h, right):
        return k < 8 or right == (h < NCH // 2)

    def sibling(k):
        for slot in {0: (0,), 8: (8,)}.get(k, (-k, k)):
            ref = sall.at[c, zmove(slot)]
            to(ref, ref, s_send, s_recv.at[max(k // 2 - 2, 0)], blk, sib).start()

    def ring_step(k):
        for h in range(NCH):
            for right in (True, False):
                if on_ring(k, h, right):
                    ref = sall.at[c, zmove(-k if right else k), pl.ds(CH * h, CH)]
                    drain(ref, (r_recv if right else l_recv).at[k - 1, h])
                    if k < 8 and on_ring(k + 1, h, right):
                        ring(k + 1, h, right).start()
        sibling(k)

    for h in range(NCH):
        for right in (True, False):
            ring(1, h, right).start()
    sibling(0)

    def halo_copy(dyl, ds):
        return to(
            sall.at[c, z], halo.at[2 - 2 * ds + yl], h_send, h_recv, lax.rem(yl + dyl, 2) * NZ + z, s + ds
        )

    for ds in (0, -1, 1):
        for dyl in (0, 1):
            if ds == 0:
                if dyl == 1:
                    halo_copy(dyl, ds).start()
            else:
                pl.when(jnp.logical_and(s + ds >= 0, s + ds < NR))(
                    lambda dyl=dyl, ds=ds: halo_copy(dyl, ds).start()
                )
    halo[2 + yl] = sall[c, z]

    useful = jnp.logical_or(odd == 0, lax.rem(s, 2) == 0)
    kind = jnp.where(odd == 1, 0, jnp.where(s < 8, 1, 2))
    part = jnp.where(odd == 1, s // 2, lax.rem(s, 8))
    shift = jnp.where(odd == 1, 1, jnp.where(s < 8, 0, -1))
    col = jnp.clip(yl * 8 + z // 2 + shift, 0, NR - 1)
    drain(raw.at[0:15], t_recv)

    @pl.when(useful)
    def _():
        own_c, rank_c = codes_of(raw, col)
        slices = raw[:, 0:16, :].reshape(256, 128)
        picked = jnp.dot(slices, onehot(rank_c, 128), preferred_element_type=F32)
        kept = jnp.zeros((16, ND), F32)
        for d in range(NR):
            kept = jnp.where(own_c == float(d), picked[16 * d : 16 * d + 16, :], kept)
        mz[z // 4] = kept.astype(BF16)
        for k in (8, 4, -4):
            to(mz.at[z // 4], mz.at[z // 4], a_send, a_recv, yl * NZ + zmove(k), s).start()

    ring_step(1)
    ring_step(2)

    def spread(f_remote, f_local):
        def each(m, carry):
            cc = yl * 8 + (lax.rem(z, 4) + 4 * m) // 2 + shift
            fits = jnp.logical_and(useful, jnp.logical_and(cc >= 0, cc < NR))
            dst = cbuf.at[kind, part]
            for dyl in range(2):
                here = jnp.logical_and(cc == s, dyl == 0)
                pl.when(jnp.logical_and(fits, jnp.logical_not(here)))(
                    lambda dyl=dyl: f_remote(
                        to(mz.at[m], dst, c_send.at[m, dyl], c_recv, lax.rem(yl + dyl, 2) * NZ + z, cc)
                    )
                )
                if f_local is not None and dyl == 0:
                    pl.when(jnp.logical_and(fits, here))(
                        lambda: f_local(pltpu.make_async_copy(mz.at[m], dst, c_recv))
                    )
            return carry

        lax.fori_loop(0, 4, each, 0)

    pl.when(useful)(lambda: drain(mz.at[0:3], a_recv))
    spread(lambda copy: copy.start(), lambda copy: copy.start())
    ring_step(3)
    ring_step(4)

    got = jnp.where(lax.rem(z, 2) == 0, jnp.where(lax.rem(z - 2 * s + 64, 4) == 0, 1, 2), 0)
    has = jnp.logical_and(
        jnp.logical_or(lax.rem(z, 2) == 0, lax.rem(z - 2 * s + 65, 4) == 0),
        jnp.logical_and(jnp.logical_or(got != 0, s > 0), jnp.logical_or(got != 2, s < NR - 1)),
    )
    got = jnp.where(has, got, 3)

    @pl.when(has)
    def _():
        drain(cbuf.at[0], c_recv)
        for k in (2, 1, -1):
            to(cbuf.at[got], cbuf.at[got], b_send, b_recv.at[got], yl * NZ + zmove(k), s).start()

    ring_step(5)

    acc[...] = jnp.zeros_like(acc)
    own_s, _ = codes_of(raw, s)
    hot_s = onehot(own_s, NR)
    edge = jnp.logical_or(s == 0, s == NR - 1)
    pl.when(edge)(lambda: drain(halo.at[0:3], h_recv))
    pl.when(jnp.logical_not(edge))(lambda: drain(halo.at[0:5], h_recv))

    def weigh(j):
        @pl.when(jnp.logical_and(s - 1 + j >= 0, s - 1 + j < NR))
        def _():
            pl.when(got != j)(lambda: drain(cbuf.at[j], b_recv.at[j]))
            own_j, rank_j = codes_of(raw, s - 1 + j)
            same = lax.dot_general(onehot(own_j, NR), hot_s, T0, preferred_element_type=F32)
            wide = lax.dot_general(onehot(rank_j, 128), cbuf[j].reshape(128, ND), T0, preferred_element_type=F32)
            m = (wide * same).astype(BF16)
            acc[...] += jnp.dot(halo[2 * j : 2 * j + 2].reshape(2 * SD, ND), m, preferred_element_type=F32)

    weigh(0)
    weigh(1)
    weigh(2)
    wown[...] = acc[...].reshape(2, SD, ND).astype(BF16)
    to(wown.at[1 - c], wc.at[c], w_send, w_recv, blk, sib).start()
    wc[c] = wown[c]
    ring_step(6)
    drain(wc.at[0], w_recv)

    def tile(d):
        u = lax.rem(z // 2 + d + 8, 8)
        pair = pl.ds(2 * u, 2)
        g = lax.dot_general(sall[0, pair].reshape(2 * SD, ND), wc[0], T1, preferred_element_type=F32)
        g += lax.dot_general(sall[1, pair].reshape(2 * SD, ND), wc[1], T1, preferred_element_type=F32)
        encode(g, gt, u)
        late = 0 if -2 <= d < 2 else 1
        home = x * 4 + lax.rem(u, 4)
        dst = yrecv.at[yl, yh, u // 4]
        far = jnp.logical_or(home != s, c != yl)
        pl.when(far)(lambda: to(gt.at[u], dst, y_send, y_recv.at[late], c * NZ + z, home).start())
        pl.when(jnp.logical_not(far))(lambda: pltpu.make_async_copy(gt.at[u], dst, y_recv.at[late]).start())

    drain(sall.at[0, 0:11], s_recv.at[0])
    for d in (0, -1, 1, -2, 2):
        tile(d)
    ring_step(7)
    drain(sall.at[0, 0:4], s_recv.at[1])
    tile(-3)
    tile(3)
    ring_step(8)
    drain(sall.at[0, 0:1], s_recv.at[2])
    tile(4)

    first = jnp.where(lax.rem(2 * yh + c - z // 2 + 10, 8) < 4, 0, 1)
    for late in range(2):
        i = lax.rem(first + late, 2)
        drain(yrecv.at[0, :, 0:2], y_recv.at[late])
        for y in range(2):
            dest = 2 * y + i
            total = decode(yrecv[y, 0, i]) + decode(yrecv[y, 1, i])

            @pl.when(x == dest)
            def _():
                xown[...] = total

            @pl.when(x != dest)
            def _():
                encode(total, xsend, dest)
                to(xsend.at[dest], xrecv.at[x], x_send, x_recv, blk, 4 * dest + 2 * yh + c).start()

    drain(xrecv.at[0:3], x_recv)
    total = xown[...]
    for k in range(1, 4):
        total += decode(xrecv[lax.rem(x + k, 4)])
    out[...] = total

    drain(msg.at[0:15], t_send)
    pl.when(useful)(lambda: drain(mz.at[0:3], a_send))
    spread(lambda copy: copy.wait_send(), None)
    pl.when(has)(lambda: drain(cbuf, b_send))
    pl.when(edge)(lambda: drain(halo.at[0:3], h_send))
    pl.when(jnp.logical_not(edge))(lambda: drain(halo.at[0:5], h_send))
    drain(sall.at[0, 0:15], z_send)
    drain(sall.at[0], s_send)
    drain(wc.at[0], w_send)
    pl.when(c == yl)(lambda: drain(gt.at[0:6], y_send))
    pl.when(c != yl)(lambda: drain(gt, y_send))
    drain(xsend.at[0:3], x_send)


def per_device(snapshots, node_owner, mass_blocks, mass_cols):
    dma = pltpu.SemaphoreType.DMA
    one = dma(())
    return pl.pallas_call(
        kernel,
        out_shape=jax.ShapeDtypeStruct((256, 128), F32),
        in_specs=[pl.BlockSpec(memory_space=pl.ANY)] * 3,
        out_specs=pl.BlockSpec(memory_space=pltpu.VMEM),
        scratch_shapes=[
            pltpu.VMEM((1, ND), jnp.int32),
            pltpu.VMEM((16, 16, 128), BF16),
            pltpu.VMEM((16, 32, 128), BF16),
            pltpu.VMEM((16, 32, 128), BF16),
            pltpu.VMEM((4, 16, ND), BF16),
            pltpu.VMEM((3, 8, 16, ND), BF16),
            pltpu.VMEM((6, SD, ND), BF16),
            pltpu.VMEM((2, NZ, SD, ND), BF16),
            pltpu.VMEM((2 * SD, ND), F32),
            pltpu.VMEM((2, SD, ND), BF16),
            pltpu.VMEM((2, SD, ND), BF16),
            pltpu.VMEM((8, 272, 128), jnp.int16),
            pltpu.VMEM((2, 2, 2, 272, 128), jnp.int16),
            pltpu.VMEM((4, 272, 128), jnp.int16),
            pltpu.VMEM((4, 272, 128), jnp.int16),
            pltpu.VMEM((256, 128), F32),
            dma((3,)), one, one, one, one, one, dma((3,)), dma((4, 2)), one,
            one, one, one, dma((8, NCH)), dma((8, NCH)), one, dma((3,)),
            one, one, one, dma((2,)), one, one,
        ],
        compiler_params=pltpu.CompilerParams(
            collective_id=0, has_side_effects=True, vmem_limit_bytes=64 * 1024 * 1024 - 64 * 1024
        ),
        cost_estimate=pl.CostEstimate(flops=1200000000, bytes_accessed=400000, transcendentals=0),
    )(snapshots, node_owner.reshape(1, ND), mass_blocks.reshape(16, 16, 128))


def solution(mesh):
    placed = (P("blk", "rows"), P("rows", None), P("rows", "blk", None, None), P("rows", "blk"))
    return jax.shard_map(
        per_device, mesh=mesh, in_specs=placed, out_specs=P("rows", "blk"), check_vma=False
    )
```

```python
import jax
import jax.numpy as jnp
from jax import lax
from jax.experimental import pallas as pl
from jax.experimental.pallas import tpu as pltpu
from jax.sharding import PartitionSpec as P

MESH = pl.DeviceIdType.MESH
F32 = jnp.float32
BF16 = jnp.bfloat16
NZ = 16
NR = 16
ND = 512
SD = 128
NCH = 4
CH = SD // NCH
FULL = 32767.0
T0 = (((0,), (0,)), ((), ()))
T1 = (((1,), (1,)), ((), ()))


def codes_of(raw, q):
    v = raw[q, 16:32, :].astype(F32)
    own = jnp.concatenate([v[i : i + 1, :] for i in range(4)], axis=1)
    rank = jnp.concatenate([v[i : i + 1, :] for i in range(4, 8)], axis=1)
    return own, rank


def onehot(row, n):
    ids = lax.broadcasted_iota(jnp.int32, (n, row.shape[1]), 0).astype(F32)
    return jnp.where(ids == row, 1.0, 0.0).astype(BF16)


def encode(g, ref, *at):
    top = jnp.clip(jnp.max(jnp.abs(g), axis=0, keepdims=True), 1e-30, 1e30)
    e = jnp.ceil(jnp.log2(top))
    q = jnp.round(g * (FULL * jnp.exp2(-e)))
    ref[(*at, slice(0, 256), slice(None))] = q.astype(jnp.int32).astype(jnp.int16)
    ref[(*at, slice(256, 272), slice(None))] = jnp.broadcast_to(e, (16, 128)).astype(jnp.int32).astype(jnp.int16)


def decode(v):
    e = v[256:272, :].astype(jnp.int32).astype(F32)[0:1, :]
    return v[0:256, :].astype(jnp.int32).astype(F32) * (jnp.exp2(e) * (1.0 / FULL))


def kernel(
    snap, owner, mass, out,
    own_v, mass_v, msg, raw, mz, cbuf, halo, sall, acc, wown, wc, gt, yrecv, xsend, xrecv, xown,
    i_sem, t_send, t_recv, a_send, a_recv, b_send, b_recv, c_send, c_recv,
    h_send, h_recv, z_send, r_recv, l_recv, s_send, s_recv,
    w_send, w_recv, y_send, y_recv, x_send, x_recv, f_sem,
):
    blk, s = lax.axis_index("blk"), lax.axis_index("rows")
    yl, z = blk // NZ, lax.rem(blk, NZ)
    x, yh, c = s // 4, lax.rem(s // 2, 2), lax.rem(s, 2)
    sib = s + 1 - 2 * c

    def zmove(k):
        return lax.rem(z + k + NZ, NZ)

    def to(src, dst, ssem, rsem, b, r):
        return pltpu.make_async_remote_copy(
            src_ref=src, dst_ref=dst, send_sem=ssem, recv_sem=rsem, device_id=(b, r), device_id_type=MESH
        )

    def drain(ref, sem):
        pltpu.make_async_copy(ref, ref, sem).wait()

    barrier = pltpu.get_barrier_semaphore()
    for k in (2, -2, 1, -1):
        pl.semaphore_signal(barrier, inc=1, device_id=(yl * NZ + zmove(k), s), device_id_type=MESH)
    plane = yl * NR + s

    def greet(i, carry):
        other = lax.rem(plane + i, 2 * NR)
        pl.semaphore_signal(
            barrier, inc=1, device_id=((other // NR) * NZ + z, lax.rem(other, NR)), device_id_type=MESH
        )
        return carry

    lax.fori_loop(1, 2 * NR, greet, 0)

    in_own = pltpu.make_async_copy(owner, own_v, i_sem.at[0])
    in_mass = pltpu.make_async_copy(mass, mass_v, i_sem.at[1])
    in_snap = pltpu.make_async_copy(snap, sall.at[c, z], i_sem.at[2])
    in_own.start()
    in_mass.start()
    in_snap.start()

    before = jnp.where(
        lax.broadcasted_iota(jnp.int32, (ND, ND), 0) < lax.broadcasted_iota(jnp.int32, (ND, ND), 1), 1.0, 0.0
    ).astype(BF16)
    in_own.wait()
    own = own_v[...].astype(F32)
    mine = onehot(own, NR)
    counts = jnp.dot(mine, before, preferred_element_type=F32)
    rank = jnp.sum(mine.astype(F32) * counts, axis=0, keepdims=True)
    row = lax.broadcasted_iota(jnp.int32, (16, 128), 0)
    code = jnp.zeros((16, 128), F32)
    for i in range(4):
        code = jnp.where(row == i, own[:, 128 * i : 128 * i + 128], code)
        code = jnp.where(row == i + 4, rank[:, 128 * i : 128 * i + 128], code)
    code = code.astype(BF16)
    odd = lax.rem(z, 2)
    in_mass.wait()
    for a in range(NR):
        msg[a, 0:16, :] = mass_v[jnp.where(odd == 1, a // 2, a)]
        msg[a, 16:32, :] = code
    raw[s] = msg[s]
    in_snap.wait()

    pl.semaphore_wait(barrier, 2 * NR - 1 + 4)

    def round_signal(n):
        for k in (2, -2):
            pl.semaphore_signal(f_sem.at[n], inc=1, device_id=(yl * NZ + zmove(k), s), device_id_type=MESH)

    def round_wait(n):
        pl.semaphore_wait(f_sem.at[n], 2)

    round_signal(0)

    def scatter(i, carry):
        a = lax.rem(s + i, NR)
        to(msg.at[a], raw.at[s], t_send, t_recv, blk, a).start()
        return carry

    lax.fori_loop(1, NR, scatter, 0)

    def ring(k, h, right):
        ref = sall.at[c, zmove(1 - k if right else k - 1), pl.ds(CH * h, CH)]
        rs = r_recv if right else l_recv
        return to(ref, ref, z_send, rs.at[k - 1, h], yl * NZ + zmove(1 if right else -1), s)

    def on_ring(k, h, right):
        return k < 8 or right == (h < NCH // 2)

    def sibling(k):
        for slot in {0: (0,), 8: (8,)}.get(k, (-k, k)):
            ref = sall.at[c, zmove(slot)]
            to(ref, ref, s_send, s_recv.at[max(k // 2 - 2, 0)], blk, sib).start()

    def ring_step(k):
        for h in range(NCH):
            for right in (True, False):
                if on_ring(k, h, right):
                    ref = sall.at[c, zmove(-k if right else k), pl.ds(CH * h, CH)]
                    drain(ref, (r_recv if right else l_recv).at[k - 1, h])
                    if k < 8 and on_ring(k + 1, h, right):
                        ring(k + 1, h, right).start()
        sibling(k)

    for h in range(NCH):
        for right in (True, False):
            ring(1, h, right).start()
    sibling(0)

    def halo_copy(dyl, ds):
        return to(
            sall.at[c, z], halo.at[2 - 2 * ds + yl], h_send, h_recv, lax.rem(yl + dyl, 2) * NZ + z, s + ds
        )

    for ds in (0, -1, 1):
        for dyl in (0, 1):
            if ds == 0:
                if dyl == 1:
                    halo_copy(dyl, ds).start()
            else:
                pl.when(jnp.logical_and(s + ds >= 0, s + ds < NR))(
                    lambda dyl=dyl, ds=ds: halo_copy(dyl, ds).start()
                )
    halo[2 + yl] = sall[c, z]
    round_wait(0)
    round_signal(1)

    useful = jnp.logical_or(odd == 0, lax.rem(s, 2) == 0)
    kind = jnp.where(odd == 1, 0, jnp.where(s < 8, 1, 2))
    part = jnp.where(odd == 1, s // 2, lax.rem(s, 8))
    shift = jnp.where(odd == 1, 1, jnp.where(s < 8, 0, -1))
    col = jnp.clip(yl * 8 + z // 2 + shift, 0, NR - 1)
    round_wait(1)
    round_signal(2)
    ring_step(1)
    drain(raw.at[0:15], t_recv)

    round_wait(2)

    @pl.when(useful)
    def _():
        own_c, rank_c = codes_of(raw, col)
        slices = raw[:, 0:16, :].reshape(256, 128)
        picked = jnp.dot(slices, onehot(rank_c, 128), preferred_element_type=F32)
        kept = jnp.zeros((16, ND), F32)
        for d in range(NR):
            kept = jnp.where(own_c == float(d), picked[16 * d : 16 * d + 16, :], kept)
        mz[z // 4] = kept.astype(BF16)
        for k in (8, 4, -4):
            to(mz.at[z // 4], mz.at[z // 4], a_send, a_recv, yl * NZ + zmove(k), s).start()

    ring_step(2)
    ring_step(3)

    def spread(f_remote, f_local):
        def each(m, carry):
            cc = yl * 8 + (lax.rem(z, 4) + 4 * m) // 2 + shift
            fits = jnp.logical_and(useful, jnp.logical_and(cc >= 0, cc < NR))
            dst = cbuf.at[kind, part]
            for dyl in range(2):
                here = jnp.logical_and(cc == s, dyl == 0)
                pl.when(jnp.logical_and(fits, jnp.logical_not(here)))(
                    lambda dyl=dyl: f_remote(
                        to(mz.at[m], dst, c_send.at[m, dyl], c_recv, lax.rem(yl + dyl, 2) * NZ + z, cc)
                    )
                )
                if f_local is not None and dyl == 0:
                    pl.when(jnp.logical_and(fits, here))(
                        lambda: f_local(pltpu.make_async_copy(mz.at[m], dst, c_recv))
                    )
            return carry

        lax.fori_loop(0, 4, each, 0)

    pl.when(useful)(lambda: drain(mz.at[0:3], a_recv))
    spread(lambda copy: copy.start(), lambda copy: copy.start())
    ring_step(4)

    got = jnp.where(lax.rem(z, 2) == 0, jnp.where(lax.rem(z - 2 * s + 64, 4) == 0, 1, 2), 0)
    has = jnp.logical_and(
        jnp.logical_or(lax.rem(z, 2) == 0, lax.rem(z - 2 * s + 65, 4) == 0),
        jnp.logical_and(jnp.logical_or(got != 0, s > 0), jnp.logical_or(got != 2, s < NR - 1)),
    )
    got = jnp.where(has, got, 3)

    @pl.when(has)
    def _():
        drain(cbuf.at[0], c_recv)
        for k in (2, 1, -1):
            to(cbuf.at[got], cbuf.at[got], b_send, b_recv.at[got], yl * NZ + zmove(k), s).start()

    ring_step(5)

    acc[...] = jnp.zeros_like(acc)
    own_s, _ = codes_of(raw, s)
    hot_s = onehot(own_s, NR)
    edge = jnp.logical_or(s == 0, s == NR - 1)
    pl.when(edge)(lambda: drain(halo.at[0:3], h_recv))
    pl.when(jnp.logical_not(edge))(lambda: drain(halo.at[0:5], h_recv))

    def weigh(j):
        @pl.when(jnp.logical_and(s - 1 + j >= 0, s - 1 + j < NR))
        def _():
            pl.when(got != j)(lambda: drain(cbuf.at[j], b_recv.at[j]))
            own_j, rank_j = codes_of(raw, s - 1 + j)
            same = lax.dot_general(onehot(own_j, NR), hot_s, T0, preferred_element_type=F32)
            wide = lax.dot_general(onehot(rank_j, 128), cbuf[j].reshape(128, ND), T0, preferred_element_type=F32)
            m = (wide * same).astype(BF16)
            acc[...] += jnp.dot(halo[pl.ds(2 * j, 2)].reshape(2 * SD, ND), m, preferred_element_type=F32)

    kinds = [lax.rem(jnp.where(has, got, 0) + n, 3) for n in range(3)]
    weigh(kinds[0])
    weigh(kinds[1])
    weigh(kinds[2])
    wown[...] = acc[...].reshape(2, SD, ND).astype(BF16)
    to(wown.at[1 - c], wc.at[c], w_send, w_recv, blk, sib).start()
    wc[c] = wown[c]
    ring_step(6)
    drain(wc.at[0], w_recv)

    def tile(d):
        u = lax.rem(z // 2 + d + 8, 8)
        pair = pl.ds(2 * u, 2)
        g = lax.dot_general(sall[0, pair].reshape(2 * SD, ND), wc[0], T1, preferred_element_type=F32)
        g += lax.dot_general(sall[1, pair].reshape(2 * SD, ND), wc[1], T1, preferred_element_type=F32)
        encode(g, gt, u)
        late = 0 if -2 <= d < 2 else 1
        home = x * 4 + lax.rem(u, 4)
        dst = yrecv.at[yl, yh, u // 4]
        far = jnp.logical_or(home != s, c != yl)
        pl.when(far)(lambda: to(gt.at[u], dst, y_send, y_recv.at[late], c * NZ + z, home).start())
        pl.when(jnp.logical_not(far))(lambda: pltpu.make_async_copy(gt.at[u], dst, y_recv.at[late]).start())

    drain(sall.at[0, 0:11], s_recv.at[0])
    for d in (0, -1, 1, -2, 2):
        tile(d)
    ring_step(7)
    drain(sall.at[0, 0:4], s_recv.at[1])
    tile(-3)
    tile(3)
    ring_step(8)
    drain(sall.at[0, 0:1], s_recv.at[2])
    tile(4)

    first = jnp.where(lax.rem(2 * yh + c - z // 2 + 10, 8) < 4, 0, 1)
    for late in range(2):
        i = lax.rem(first + late, 2)
        drain(yrecv.at[0, :, 0:2], y_recv.at[late])
        for y in range(2):
            dest = 2 * y + i
            total = decode(yrecv[y, 0, i]) + decode(yrecv[y, 1, i])

            @pl.when(x == dest)
            def _():
                xown[...] = total

            @pl.when(x != dest)
            def _():
                encode(total, xsend, dest)
                to(xsend.at[dest], xrecv.at[x], x_send, x_recv, blk, 4 * dest + 2 * yh + c).start()

    drain(xrecv.at[0:3], x_recv)
    total = xown[...]
    for k in range(1, 4):
        total += decode(xrecv[lax.rem(x + k, 4)])
    out[...] = total

    drain(msg.at[0:15], t_send)
    pl.when(useful)(lambda: drain(mz.at[0:3], a_send))
    spread(lambda copy: copy.wait_send(), None)
    pl.when(has)(lambda: drain(cbuf, b_send))
    pl.when(edge)(lambda: drain(halo.at[0:3], h_send))
    pl.when(jnp.logical_not(edge))(lambda: drain(halo.at[0:5], h_send))
    drain(sall.at[0, 0:15], z_send)
    drain(sall.at[0], s_send)
    drain(wc.at[0], w_send)
    pl.when(c == yl)(lambda: drain(gt.at[0:6], y_send))
    pl.when(c != yl)(lambda: drain(gt, y_send))
    drain(xsend.at[0:3], x_send)


def per_device(snapshots, node_owner, mass_blocks, mass_cols):
    dma = pltpu.SemaphoreType.DMA
    one = dma(())
    return pl.pallas_call(
        kernel,
        out_shape=jax.ShapeDtypeStruct((256, 128), F32),
        in_specs=[pl.BlockSpec(memory_space=pl.ANY)] * 3,
        out_specs=pl.BlockSpec(memory_space=pltpu.VMEM),
        scratch_shapes=[
            pltpu.VMEM((1, ND), jnp.int32),
            pltpu.VMEM((16, 16, 128), BF16),
            pltpu.VMEM((16, 32, 128), BF16),
            pltpu.VMEM((16, 32, 128), BF16),
            pltpu.VMEM((4, 16, ND), BF16),
            pltpu.VMEM((3, 8, 16, ND), BF16),
            pltpu.VMEM((6, SD, ND), BF16),
            pltpu.VMEM((2, NZ, SD, ND), BF16),
            pltpu.VMEM((2 * SD, ND), F32),
            pltpu.VMEM((2, SD, ND), BF16),
            pltpu.VMEM((2, SD, ND), BF16),
            pltpu.VMEM((8, 272, 128), jnp.int16),
            pltpu.VMEM((2, 2, 2, 272, 128), jnp.int16),
            pltpu.VMEM((4, 272, 128), jnp.int16),
            pltpu.VMEM((4, 272, 128), jnp.int16),
            pltpu.VMEM((256, 128), F32),
            dma((3,)), one, one, one, one, one, dma((3,)), dma((4, 2)), one,
            one, one, one, dma((8, NCH)), dma((8, NCH)), one, dma((3,)),
            one, one, one, dma((2,)), one, one, pltpu.SemaphoreType.REGULAR((3,)),
        ],
        compiler_params=pltpu.CompilerParams(
            collective_id=0, has_side_effects=True, vmem_limit_bytes=64 * 1024 * 1024 - 64 * 1024
        ),
        cost_estimate=pl.CostEstimate(flops=1200000000, bytes_accessed=400000, transcendentals=0),
    )(snapshots, node_owner.reshape(1, ND), mass_blocks.reshape(16, 16, 128))


def solution(mesh):
    placed = (P("blk", "rows"), P("rows", None), P("rows", "blk", None, None), P("rows", "blk"))
    return jax.shard_map(
        per_device, mesh=mesh, in_specs=placed, out_specs=P("rows", "blk"), check_vma=False
    )
```

```python
import jax
import jax.numpy as jnp
from jax import lax
from jax.experimental import pallas as pl
from jax.experimental.pallas import tpu as pltpu
from jax.sharding import PartitionSpec as P

MESH = pl.DeviceIdType.MESH
F32 = jnp.float32
BF16 = jnp.bfloat16
NZ = 16
NR = 16
ND = 512
SD = 128
NCH = 4
CH = SD // NCH
FULL = 32767.0
T0 = (((0,), (0,)), ((), ()))
T1 = (((1,), (1,)), ((), ()))


def codes_of(raw, q):
    v = raw[q, 16:32, :].astype(F32)
    own = jnp.concatenate([v[i : i + 1, :] for i in range(4)], axis=1)
    rank = jnp.concatenate([v[i : i + 1, :] for i in range(4, 8)], axis=1)
    return own, rank


def onehot(row, n):
    ids = lax.broadcasted_iota(jnp.int32, (n, row.shape[1]), 0).astype(F32)
    return jnp.where(ids == row, 1.0, 0.0).astype(BF16)


def encode(g, ref, *at):
    top = jnp.clip(jnp.max(jnp.abs(g), axis=0, keepdims=True), 1e-30, 1e30)
    e = jnp.ceil(jnp.log2(top))
    q = jnp.round(g * (FULL * jnp.exp2(-e)))
    ref[(*at, slice(0, 256), slice(None))] = q.astype(jnp.int32).astype(jnp.int16)
    ref[(*at, slice(256, 272), slice(None))] = jnp.broadcast_to(e, (16, 128)).astype(jnp.int32).astype(jnp.int16)


def decode(v):
    e = v[256:272, :].astype(jnp.int32).astype(F32)[0:1, :]
    return v[0:256, :].astype(jnp.int32).astype(F32) * (jnp.exp2(e) * (1.0 / FULL))


def kernel(
    snap, owner, mass, out,
    own_v, mass_v, msg, raw, mz, cbuf, halo, sall, acc, wown, wc, gt, yrecv, xsend, xrecv, xown,
    i_sem, t_send, t_recv, a_send, a_recv, c_send, c_recv,
    h_send, h_recv, z_send, r_recv, l_recv, s_send, s_recv,
    w_send, w_recv, y_send, y_recv, x_send, x_recv, f_sem,
):
    blk, s = lax.axis_index("blk"), lax.axis_index("rows")
    yl, z = blk // NZ, lax.rem(blk, NZ)
    x, yh, c = s // 4, lax.rem(s // 2, 2), lax.rem(s, 2)
    sib = s + 1 - 2 * c

    def zmove(k):
        return lax.rem(z + k + NZ, NZ)

    def to(src, dst, ssem, rsem, b, r):
        return pltpu.make_async_remote_copy(
            src_ref=src, dst_ref=dst, send_sem=ssem, recv_sem=rsem, device_id=(b, r), device_id_type=MESH
        )

    def drain(ref, sem):
        pltpu.make_async_copy(ref, ref, sem).wait()

    barrier = pltpu.get_barrier_semaphore()
    for k in (2, -2, 1, -1):
        pl.semaphore_signal(barrier, inc=1, device_id=(yl * NZ + zmove(k), s), device_id_type=MESH)
    plane = yl * NR + s

    def greet(i, carry):
        other = lax.rem(plane + i, 2 * NR)
        pl.semaphore_signal(
            barrier, inc=1, device_id=((other // NR) * NZ + z, lax.rem(other, NR)), device_id_type=MESH
        )
        return carry

    lax.fori_loop(1, 2 * NR, greet, 0)

    in_own = pltpu.make_async_copy(owner, own_v, i_sem.at[0])
    in_mass = pltpu.make_async_copy(mass, mass_v, i_sem.at[1])
    in_snap = pltpu.make_async_copy(snap, sall.at[c, z], i_sem.at[2])
    in_own.start()
    in_mass.start()
    in_snap.start()

    before = jnp.where(
        lax.broadcasted_iota(jnp.int32, (ND, ND), 0) < lax.broadcasted_iota(jnp.int32, (ND, ND), 1), 1.0, 0.0
    ).astype(BF16)
    in_own.wait()
    own = own_v[...].astype(F32)
    mine = onehot(own, NR)
    counts = jnp.dot(mine, before, preferred_element_type=F32)
    rank = jnp.sum(mine.astype(F32) * counts, axis=0, keepdims=True)
    row = lax.broadcasted_iota(jnp.int32, (16, 128), 0)
    code = jnp.zeros((16, 128), F32)
    for i in range(4):
        code = jnp.where(row == i, own[:, 128 * i : 128 * i + 128], code)
        code = jnp.where(row == i + 4, rank[:, 128 * i : 128 * i + 128], code)
    code = code.astype(BF16)
    odd = lax.rem(z, 2)
    in_mass.wait()
    for a in range(NR):
        msg[a, 0:16, :] = mass_v[jnp.where(odd == 1, a // 2, a)]
        msg[a, 16:32, :] = code
    raw[s] = msg[s]
    in_snap.wait()

    pl.semaphore_wait(barrier, 2 * NR - 1 + 4)

    def round_signal(n):
        for k in (2, -2, 1, -1) if n == 0 else (2, -2):
            pl.semaphore_signal(f_sem.at[n], inc=1, device_id=(yl * NZ + zmove(k), s), device_id_type=MESH)

    def round_wait(n):
        pl.semaphore_wait(f_sem.at[n], 4 if n == 0 else 2)

    round_signal(0)

    def scatter(i, carry):
        a = lax.rem(s + i, NR)
        to(msg.at[a], raw.at[s], t_send, t_recv, blk, a).start()
        return carry

    lax.fori_loop(1, NR, scatter, 0)

    def ring(k, h, right):
        ref = sall.at[c, zmove(1 - k if right else k - 1), pl.ds(CH * h, CH)]
        rs = r_recv if right else l_recv
        return to(ref, ref, z_send, rs.at[k - 1, h], yl * NZ + zmove(1 if right else -1), s)

    def on_ring(k, h, right):
        return k < 8 or right == (h < NCH // 2)

    def sibling(k):
        for slot in {0: (0,), 8: (8,)}.get(k, (-k, k)):
            ref = sall.at[c, zmove(slot)]
            to(ref, ref, s_send, s_recv.at[max(k // 2 - 2, 0)], blk, sib).start()

    def ring_step(k):
        for h in range(NCH):
            for right in (True, False):
                if on_ring(k, h, right):
                    ref = sall.at[c, zmove(-k if right else k), pl.ds(CH * h, CH)]
                    drain(ref, (r_recv if right else l_recv).at[k - 1, h])
                    if k < 8 and on_ring(k + 1, h, right):
                        ring(k + 1, h, right).start()
        sibling(k)

    for h in range(NCH):
        for right in (True, False):
            ring(1, h, right).start()
    sibling(0)

    def halo_copy(dyl, ds):
        return to(
            sall.at[c, z], halo.at[2 - 2 * ds + yl], h_send, h_recv, lax.rem(yl + dyl, 2) * NZ + z, s + ds
        )

    for ds in (0, -1, 1):
        for dyl in (0, 1):
            if ds == 0:
                if dyl == 1:
                    halo_copy(dyl, ds).start()
            else:
                pl.when(jnp.logical_and(s + ds >= 0, s + ds < NR))(
                    lambda dyl=dyl, ds=ds: halo_copy(dyl, ds).start()
                )
    halo[2 + yl] = sall[c, z]
    round_wait(0)
    round_signal(1)

    useful = jnp.logical_or(odd == 0, lax.rem(s, 2) == 0)
    kind = jnp.where(odd == 1, 0, jnp.where(s < 8, 1, 2))
    part = jnp.where(odd == 1, s // 2, lax.rem(s, 8))
    shift = jnp.where(odd == 1, 1, jnp.where(s < 8, 0, -1))
    col = jnp.clip(yl * 8 + z // 2 + shift, 0, NR - 1)
    round_wait(1)
    round_signal(2)
    ring_step(1)
    drain(raw.at[0:15], t_recv)

    round_wait(2)

    @pl.when(useful)
    def _():
        own_c, rank_c = codes_of(raw, col)
        slices = raw[:, 0:16, :].reshape(256, 128)
        picked = jnp.dot(slices, onehot(rank_c, 128), preferred_element_type=F32)
        kept = jnp.zeros((16, ND), F32)
        for d in range(NR):
            kept = jnp.where(own_c == float(d), picked[16 * d : 16 * d + 16, :], kept)
        mz[z // 4] = kept.astype(BF16)
        for k in (8, 4, -4):
            to(mz.at[z // 4], mz.at[z // 4], a_send, a_recv, yl * NZ + zmove(k), s).start()

    ring_step(2)
    ring_step(3)

    def spread(f):
        def each(m, carry):
            cc = yl * 8 + (lax.rem(z, 4) + 4 * m) // 2 + shift
            pl.when(jnp.logical_and(useful, jnp.logical_and(cc >= 0, cc < NR)))(lambda: f(m, cc))
            return carry

        lax.fori_loop(0, 4, each, 0)

    def spread_start(m, cc):
        dst = cbuf.at[kind, part]
        for k in (2, 1, -1, 0):
            for dyl in (1, 0):
                copy = to(
                    mz.at[m], dst, c_send.at[m], c_recv.at[kind], lax.rem(yl + dyl, 2) * NZ + zmove(k), cc
                )
                if k == 0 and dyl == 0:
                    pl.when(cc != s)(lambda copy=copy: copy.start())
                    pl.when(cc == s)(lambda: pltpu.make_async_copy(mz.at[m], dst, c_recv.at[kind]).start())
                else:
                    copy.start()

    def spread_sent(m, cc):
        pl.when(cc == s)(lambda: drain(cbuf.at[0, 0:7], c_send.at[m]))
        pl.when(cc != s)(lambda: drain(cbuf.at[0], c_send.at[m]))

    pl.when(useful)(lambda: drain(mz.at[0:3], a_recv))
    spread(spread_start)
    ring_step(4)
    ring_step(5)

    acc[...] = jnp.zeros_like(acc)
    own_s, _ = codes_of(raw, s)
    hot_s = onehot(own_s, NR)
    edge = jnp.logical_or(s == 0, s == NR - 1)
    pl.when(edge)(lambda: drain(halo.at[0:3], h_recv))
    pl.when(jnp.logical_not(edge))(lambda: drain(halo.at[0:5], h_recv))

    def weigh(j):
        @pl.when(jnp.logical_and(s - 1 + j >= 0, s - 1 + j < NR))
        def _():
            drain(cbuf.at[j], c_recv.at[j])
            own_j, rank_j = codes_of(raw, s - 1 + j)
            same = lax.dot_general(onehot(own_j, NR), hot_s, T0, preferred_element_type=F32)
            wide = lax.dot_general(onehot(rank_j, 128), cbuf[j].reshape(128, ND), T0, preferred_element_type=F32)
            m = (wide * same).astype(BF16)
            acc[...] += jnp.dot(halo[pl.ds(2 * j, 2)].reshape(2 * SD, ND), m, preferred_element_type=F32)

    weigh(0)
    weigh(1)
    weigh(2)
    wown[...] = acc[...].reshape(2, SD, ND).astype(BF16)
    to(wown.at[1 - c], wc.at[c], w_send, w_recv, blk, sib).start()
    wc[c] = wown[c]
    ring_step(6)
    drain(wc.at[0], w_recv)

    def tile(d):
        u = lax.rem(z // 2 + d + 8, 8)
        pair = pl.ds(2 * u, 2)
        g = lax.dot_general(sall[0, pair].reshape(2 * SD, ND), wc[0], T1, preferred_element_type=F32)
        g += lax.dot_general(sall[1, pair].reshape(2 * SD, ND), wc[1], T1, preferred_element_type=F32)
        encode(g, gt, u)
        late = 0 if -2 <= d < 2 else 1
        home = x * 4 + lax.rem(u, 4)
        dst = yrecv.at[yl, yh, u // 4]
        far = jnp.logical_or(home != s, c != yl)
        pl.when(far)(lambda: to(gt.at[u], dst, y_send, y_recv.at[late], c * NZ + z, home).start())
        pl.when(jnp.logical_not(far))(lambda: pltpu.make_async_copy(gt.at[u], dst, y_recv.at[late]).start())

    drain(sall.at[0, 0:11], s_recv.at[0])
    for d in (0, -1, 1, -2, 2):
        tile(d)
    ring_step(7)
    drain(sall.at[0, 0:4], s_recv.at[1])
    tile(-3)
    tile(3)
    ring_step(8)
    drain(sall.at[0, 0:1], s_recv.at[2])
    tile(4)

    first = jnp.where(lax.rem(2 * yh + c - z // 2 + 10, 8) < 4, 0, 1)
    for late in range(2):
        i = lax.rem(first + late, 2)
        drain(yrecv.at[0, :, 0:2], y_recv.at[late])
        for y in range(2):
            dest = 2 * y + i
            total = decode(yrecv[y, 0, i]) + decode(yrecv[y, 1, i])

            @pl.when(x == dest)
            def _():
                xown[...] = total

            @pl.when(x != dest)
            def _():
                encode(total, xsend, dest)
                to(xsend.at[dest], xrecv.at[x], x_send, x_recv, blk, 4 * dest + 2 * yh + c).start()

    drain(xrecv.at[0:3], x_recv)
    total = xown[...]
    for k in range(1, 4):
        total += decode(xrecv[lax.rem(x + k, 4)])
    out[...] = total

    drain(msg.at[0:15], t_send)
    pl.when(useful)(lambda: drain(mz.at[0:3], a_send))
    spread(spread_sent)
    pl.when(edge)(lambda: drain(halo.at[0:3], h_send))
    pl.when(jnp.logical_not(edge))(lambda: drain(halo.at[0:5], h_send))
    drain(sall.at[0, 0:15], z_send)
    drain(sall.at[0], s_send)
    drain(wc.at[0], w_send)
    pl.when(c == yl)(lambda: drain(gt.at[0:6], y_send))
    pl.when(c != yl)(lambda: drain(gt, y_send))
    drain(xsend.at[0:3], x_send)


def per_device(snapshots, node_owner, mass_blocks, mass_cols):
    dma = pltpu.SemaphoreType.DMA
    one = dma(())
    return pl.pallas_call(
        kernel,
        out_shape=jax.ShapeDtypeStruct((256, 128), F32),
        in_specs=[pl.BlockSpec(memory_space=pl.ANY)] * 3,
        out_specs=pl.BlockSpec(memory_space=pltpu.VMEM),
        scratch_shapes=[
            pltpu.VMEM((1, ND), jnp.int32),
            pltpu.VMEM((16, 16, 128), BF16),
            pltpu.VMEM((16, 32, 128), BF16),
            pltpu.VMEM((16, 32, 128), BF16),
            pltpu.VMEM((4, 16, ND), BF16),
            pltpu.VMEM((3, 8, 16, ND), BF16),
            pltpu.VMEM((6, SD, ND), BF16),
            pltpu.VMEM((2, NZ, SD, ND), BF16),
            pltpu.VMEM((2 * SD, ND), F32),
            pltpu.VMEM((2, SD, ND), BF16),
            pltpu.VMEM((2, SD, ND), BF16),
            pltpu.VMEM((8, 272, 128), jnp.int16),
            pltpu.VMEM((2, 2, 2, 272, 128), jnp.int16),
            pltpu.VMEM((4, 272, 128), jnp.int16),
            pltpu.VMEM((4, 272, 128), jnp.int16),
            pltpu.VMEM((256, 128), F32),
            dma((3,)), one, one, one, one, dma((4,)), dma((3,)),
            one, one, one, dma((8, NCH)), dma((8, NCH)), one, dma((3,)),
            one, one, one, dma((2,)), one, one, pltpu.SemaphoreType.REGULAR((3,)),
        ],
        compiler_params=pltpu.CompilerParams(
            collective_id=0, has_side_effects=True, vmem_limit_bytes=64 * 1024 * 1024 - 64 * 1024
        ),
        cost_estimate=pl.CostEstimate(flops=1200000000, bytes_accessed=400000, transcendentals=0),
    )(snapshots, node_owner.reshape(1, ND), mass_blocks.reshape(16, 16, 128))


def solution(mesh):
    placed = (P("blk", "rows"), P("rows", None), P("rows", "blk", None, None), P("rows", "blk"))
    return jax.shard_map(
        per_device, mesh=mesh, in_specs=placed, out_specs=P("rows", "blk"), check_vma=False
    )
```

```python
import jax
import jax.numpy as jnp
from jax import lax
from jax.experimental import pallas as pl
from jax.experimental.pallas import tpu as pltpu
from jax.sharding import PartitionSpec as P

MESH = pl.DeviceIdType.MESH
F32 = jnp.float32
BF16 = jnp.bfloat16
NZ = 16
NR = 16
ND = 512
SD = 128
NCH = 4
CH = SD // NCH
FULL = 32767.0
T0 = (((0,), (0,)), ((), ()))
T1 = (((1,), (1,)), ((), ()))


def codes_of(raw, q):
    v = raw[q, 16:32, :].astype(F32)
    own = jnp.concatenate([v[i : i + 1, :] for i in range(4)], axis=1)
    rank = jnp.concatenate([v[i : i + 1, :] for i in range(4, 8)], axis=1)
    return own, rank


def onehot(row, n):
    ids = lax.broadcasted_iota(jnp.int32, (n, row.shape[1]), 0).astype(F32)
    return jnp.where(ids == row, 1.0, 0.0).astype(BF16)


def encode(g, ref, *at):
    top = jnp.clip(jnp.max(jnp.abs(g), axis=0, keepdims=True), 1e-30, 1e30)
    e = jnp.ceil(jnp.log2(top))
    q = jnp.round(g * (FULL * jnp.exp2(-e)))
    ref[(*at, slice(0, 256), slice(None))] = q.astype(jnp.int32).astype(jnp.int16)
    ref[(*at, slice(256, 272), slice(None))] = jnp.broadcast_to(e, (16, 128)).astype(jnp.int32).astype(jnp.int16)


def decode(v):
    e = v[256:272, :].astype(jnp.int32).astype(F32)[0:1, :]
    return v[0:256, :].astype(jnp.int32).astype(F32) * (jnp.exp2(e) * (1.0 / FULL))


def kernel(
    snap, owner, mass, out,
    own_v, mass_v, msg, raw, mz, cbuf, halo, sall, acc, wown, wc, gt, yrecv, xsend, xrecv, xown, drecv,
    i_sem, t_send, t_recv, a_send, a_recv, c_send, c_recv,
    h_send, h_recv, z_send, r_recv, l_recv, s_send, s_recv,
    w_send, w_recv, y_send, y_recv, x_send, x_recv, f_sem, d_send, d_recv,
):
    blk, s = lax.axis_index("blk"), lax.axis_index("rows")
    yl, z = blk // NZ, lax.rem(blk, NZ)
    x, yh, c = s // 4, lax.rem(s // 2, 2), lax.rem(s, 2)
    sib = s + 1 - 2 * c

    def zmove(k):
        return lax.rem(z + k + NZ, NZ)

    def to(src, dst, ssem, rsem, b, r):
        return pltpu.make_async_remote_copy(
            src_ref=src, dst_ref=dst, send_sem=ssem, recv_sem=rsem, device_id=(b, r), device_id_type=MESH
        )

    def drain(ref, sem):
        pltpu.make_async_copy(ref, ref, sem).wait()

    barrier = pltpu.get_barrier_semaphore()
    for k in (2, -2, 1, -1):
        pl.semaphore_signal(barrier, inc=1, device_id=(yl * NZ + zmove(k), s), device_id_type=MESH)
    plane = yl * NR + s

    def greet(i, carry):
        other = lax.rem(plane + i, 2 * NR)
        pl.semaphore_signal(
            barrier, inc=1, device_id=((other // NR) * NZ + z, lax.rem(other, NR)), device_id_type=MESH
        )
        return carry

    lax.fori_loop(1, 2 * NR, greet, 0)

    in_own = pltpu.make_async_copy(owner, own_v, i_sem.at[0])
    in_mass = pltpu.make_async_copy(mass, mass_v, i_sem.at[1])
    in_snap = pltpu.make_async_copy(snap, sall.at[c, z], i_sem.at[2])
    in_own.start()
    in_mass.start()
    in_snap.start()

    before = jnp.where(
        lax.broadcasted_iota(jnp.int32, (ND, ND), 0) < lax.broadcasted_iota(jnp.int32, (ND, ND), 1), 1.0, 0.0
    ).astype(BF16)
    in_own.wait()
    own = own_v[...].astype(F32)
    mine = onehot(own, NR)
    counts = jnp.dot(mine, before, preferred_element_type=F32)
    rank = jnp.sum(mine.astype(F32) * counts, axis=0, keepdims=True)
    row = lax.broadcasted_iota(jnp.int32, (16, 128), 0)
    code = jnp.zeros((16, 128), F32)
    for i in range(4):
        code = jnp.where(row == i, own[:, 128 * i : 128 * i + 128], code)
        code = jnp.where(row == i + 4, rank[:, 128 * i : 128 * i + 128], code)
    code = code.astype(BF16)
    odd = lax.rem(z, 2)
    in_mass.wait()
    for a in range(NR):
        msg[a, 0:16, :] = mass_v[jnp.where(odd == 1, a // 2, a)]
        msg[a, 16:32, :] = code
    raw[s] = msg[s]
    in_snap.wait()

    pl.semaphore_wait(barrier, 2 * NR - 1 + 4)

    def round_signal(n):
        for k in (2, -2, 1, -1) if n == 0 else (2, -2):
            pl.semaphore_signal(f_sem.at[n], inc=1, device_id=(yl * NZ + zmove(k), s), device_id_type=MESH)

    def round_wait(n):
        pl.semaphore_wait(f_sem.at[n], 4 if n == 0 else 2)

    round_signal(0)

    def scatter(i, carry):
        a = lax.rem(s + i, NR)
        to(msg.at[a], raw.at[s], t_send, t_recv, blk, a).start()
        return carry

    lax.fori_loop(1, NR, scatter, 0)

    def ring(k, h, right):
        ref = sall.at[c, zmove(1 - k if right else k - 1), pl.ds(CH * h, CH)]
        rs = r_recv if right else l_recv
        return to(ref, ref, z_send, rs.at[k - 1, h], yl * NZ + zmove(1 if right else -1), s)

    def on_ring(k, h, right):
        return k < 8 or right == (h < NCH // 2)

    def sibling(k):
        for slot in {0: (0,), 8: (8,)}.get(k, (-k, k)):
            ref = sall.at[c, zmove(slot)]
            to(ref, ref, s_send, s_recv.at[max(k // 2 - 2, 0)], blk, sib).start()

    def ring_step(k):
        for h in range(NCH):
            for right in (True, False):
                if on_ring(k, h, right):
                    ref = sall.at[c, zmove(-k if right else k), pl.ds(CH * h, CH)]
                    drain(ref, (r_recv if right else l_recv).at[k - 1, h])
                    if k < 8 and on_ring(k + 1, h, right):
                        ring(k + 1, h, right).start()
        sibling(k)

    for h in range(NCH):
        for right in (True, False):
            ring(1, h, right).start()
    sibling(0)

    def halo_copy(dyl, ds):
        return to(
            sall.at[c, z], halo.at[2 - 2 * ds + yl], h_send, h_recv, lax.rem(yl + dyl, 2) * NZ + z, s + ds
        )

    for ds in (0, -1, 1):
        for dyl in (0, 1):
            if ds == 0:
                if dyl == 1:
                    halo_copy(dyl, ds).start()
            else:
                pl.when(jnp.logical_and(s + ds >= 0, s + ds < NR))(
                    lambda dyl=dyl, ds=ds: halo_copy(dyl, ds).start()
                )
    halo[2 + yl] = sall[c, z]
    round_wait(0)
    round_signal(1)

    useful = jnp.logical_or(odd == 0, lax.rem(s, 2) == 0)
    kind = jnp.where(odd == 1, 0, jnp.where(s < 8, 1, 2))
    part = jnp.where(odd == 1, s // 2, lax.rem(s, 8))
    shift = jnp.where(odd == 1, 1, jnp.where(s < 8, 0, -1))
    col = jnp.clip(yl * 8 + z // 2 + shift, 0, NR - 1)
    round_wait(1)
    round_signal(2)
    ring_step(1)
    drain(raw.at[0:15], t_recv)

    round_wait(2)

    @pl.when(useful)
    def _():
        own_c, rank_c = codes_of(raw, col)
        slices = raw[:, 0:16, :].reshape(256, 128)
        picked = jnp.dot(slices, onehot(rank_c, 128), preferred_element_type=F32)
        kept = jnp.zeros((16, ND), F32)
        for d in range(NR):
            kept = jnp.where(own_c == float(d), picked[16 * d : 16 * d + 16, :], kept)
        mz[z // 4] = kept.astype(BF16)
        for k in (8, 4, -4):
            to(mz.at[z // 4], mz.at[z // 4], a_send, a_recv, yl * NZ + zmove(k), s).start()

    ring_step(2)
    ring_step(3)

    def spread(f):
        def each(m, carry):
            cc = yl * 8 + (lax.rem(z, 4) + 4 * m) // 2 + shift
            pl.when(jnp.logical_and(useful, jnp.logical_and(cc >= 0, cc < NR)))(lambda: f(m, cc))
            return carry

        lax.fori_loop(0, 4, each, 0)

    def spread_start(m, cc):
        dst = cbuf.at[kind, part]
        for k in (2, 1, -1, 0):
            for dyl in (1, 0):
                copy = to(
                    mz.at[m], dst, c_send.at[m], c_recv.at[kind], lax.rem(yl + dyl, 2) * NZ + zmove(k), cc
                )
                if k == 0 and dyl == 0:
                    pl.when(cc != s)(lambda copy=copy: copy.start())
                    pl.when(cc == s)(lambda: pltpu.make_async_copy(mz.at[m], dst, c_recv.at[kind]).start())
                else:
                    copy.start()

    def spread_sent(m, cc):
        pl.when(cc == s)(lambda: drain(cbuf.at[0, 0:7], c_send.at[m]))
        pl.when(cc != s)(lambda: drain(cbuf.at[0], c_send.at[m]))

    pl.when(useful)(lambda: drain(mz.at[0:3], a_recv))
    spread(spread_start)
    ring_step(4)
    ring_step(5)

    acc[...] = jnp.zeros_like(acc)
    own_s, _ = codes_of(raw, s)
    hot_s = onehot(own_s, NR)
    edge = jnp.logical_or(s == 0, s == NR - 1)
    pl.when(edge)(lambda: drain(halo.at[0:3], h_recv))
    pl.when(jnp.logical_not(edge))(lambda: drain(halo.at[0:5], h_recv))

    def weigh(j):
        @pl.when(jnp.logical_and(s - 1 + j >= 0, s - 1 + j < NR))
        def _():
            drain(cbuf.at[j], c_recv.at[j])
            own_j, rank_j = codes_of(raw, s - 1 + j)
            same = lax.dot_general(onehot(own_j, NR), hot_s, T0, preferred_element_type=F32)
            wide = lax.dot_general(onehot(rank_j, 128), cbuf[j].reshape(128, ND), T0, preferred_element_type=F32)
            m = (wide * same).astype(BF16)
            acc[...] += jnp.dot(halo[pl.ds(2 * j, 2)].reshape(2 * SD, ND), m, preferred_element_type=F32)

    weigh(0)
    weigh(1)
    weigh(2)
    wown[...] = acc[...].reshape(2, SD, ND).astype(BF16)
    to(wown.at[1 - c], wc.at[c], w_send, w_recv, blk, sib).start()
    wc[c] = wown[c]
    ring_step(6)
    drain(wc.at[0], w_recv)

    def tile(d):
        u = lax.rem(z // 2 + d + 8, 8)
        pair = pl.ds(2 * u, 2)
        g = lax.dot_general(sall[0, pair].reshape(2 * SD, ND), wc[0], T1, preferred_element_type=F32)
        g += lax.dot_general(sall[1, pair].reshape(2 * SD, ND), wc[1], T1, preferred_element_type=F32)
        encode(g, gt, u)
        if d == 4:
            home, dst, ssem, rsem = (2 * yl + u // 4) * 4 + lax.rem(u, 4), drecv.at[x, yh], d_send, d_recv
        else:
            home, dst, ssem = x * 4 + lax.rem(u, 4), yrecv.at[yl, yh, u // 4], y_send
            rsem = y_recv.at[0 if -2 <= d < 2 else 1]
        far = jnp.logical_or(home != s, c != yl)
        pl.when(far)(lambda: to(gt.at[u], dst, ssem, rsem, c * NZ + z, home).start())
        pl.when(jnp.logical_not(far))(lambda: pltpu.make_async_copy(gt.at[u], dst, rsem).start())

    drain(sall.at[0, 0:11], s_recv.at[0])
    for d in (0, -1, 1, -2, 2):
        tile(d)
    ring_step(7)
    drain(sall.at[0, 0:4], s_recv.at[1])
    tile(-3)
    tile(3)
    first = jnp.where(lax.rem(2 * yh + c - z // 2 + 10, 8) < 4, 0, 1)
    last = lax.rem(z // 2, 4) == 2 * yh + c
    direct = jnp.logical_and(last, lax.rem(x + first, 2) == 1)

    def half(late):
        i = lax.rem(first + late, 2)
        drain(yrecv.at[0, :, 0:2], y_recv.at[late])
        for y in range(2):
            dest = 2 * y + i
            total = decode(yrecv[y, 0, i]) + decode(yrecv[y, 1, i])

            @pl.when(x == dest)
            def _():
                xown[...] = total

            @pl.when(x != dest)
            def _():
                encode(total, xsend, dest)
                to(xsend.at[dest], xrecv.at[x], x_send, x_recv, blk, 4 * dest + 2 * yh + c).start()

    ring_step(8)
    half(0)
    drain(sall.at[0, 0:1], s_recv.at[2])
    tile(4)

    pl.when(jnp.logical_not(last))(lambda: half(1))

    @pl.when(direct)
    def _():
        drain(drecv, d_recv)
        total = decode(drecv[0, 0]) + decode(drecv[0, 1])
        for k in range(1, 4):
            total += decode(drecv[k, 0]) + decode(drecv[k, 1])
        out[...] = total

    @pl.when(jnp.logical_not(direct))
    def _():
        drain(xrecv.at[0:3], x_recv)
        total = xown[...]
        for k in range(1, 4):
            total += decode(xrecv[lax.rem(x + k, 4)])
        out[...] = total

    drain(msg.at[0:15], t_send)
    pl.when(useful)(lambda: drain(mz.at[0:3], a_send))
    spread(spread_sent)
    pl.when(edge)(lambda: drain(halo.at[0:3], h_send))
    pl.when(jnp.logical_not(edge))(lambda: drain(halo.at[0:5], h_send))
    drain(sall.at[0, 0:15], z_send)
    drain(sall.at[0], s_send)
    drain(wc.at[0], w_send)
    own_y = c == yl
    pl.when(jnp.logical_not(own_y))(lambda: drain(gt.at[0:7], y_send))
    pl.when(jnp.logical_and(own_y, last))(lambda: drain(gt.at[0:6], y_send))
    pl.when(jnp.logical_and(own_y, jnp.logical_not(last)))(lambda: drain(gt.at[0:5], y_send))
    u_last = lax.rem(z // 2 + 4, 8)
    self_last = jnp.logical_and(own_y, (2 * yl + u_last // 4) * 4 + lax.rem(u_last, 4) == s)
    pl.when(jnp.logical_not(self_last))(lambda: drain(gt.at[0], d_send))
    pl.when(jnp.logical_not(last))(lambda: drain(xsend.at[0:3], x_send))
    pl.when(direct)(lambda: drain(xsend.at[0:2], x_send))
    pl.when(jnp.logical_and(last, jnp.logical_not(direct)))(lambda: drain(xsend.at[0], x_send))


def per_device(snapshots, node_owner, mass_blocks, mass_cols):
    dma = pltpu.SemaphoreType.DMA
    one = dma(())
    return pl.pallas_call(
        kernel,
        out_shape=jax.ShapeDtypeStruct((256, 128), F32),
        in_specs=[pl.BlockSpec(memory_space=pl.ANY)] * 3,
        out_specs=pl.BlockSpec(memory_space=pltpu.VMEM),
        scratch_shapes=[
            pltpu.VMEM((1, ND), jnp.int32),
            pltpu.VMEM((16, 16, 128), BF16),
            pltpu.VMEM((16, 32, 128), BF16),
            pltpu.VMEM((16, 32, 128), BF16),
            pltpu.VMEM((4, 16, ND), BF16),
            pltpu.VMEM((3, 8, 16, ND), BF16),
            pltpu.VMEM((6, SD, ND), BF16),
            pltpu.VMEM((2, NZ, SD, ND), BF16),
            pltpu.VMEM((2 * SD, ND), F32),
            pltpu.VMEM((2, SD, ND), BF16),
            pltpu.VMEM((2, SD, ND), BF16),
            pltpu.VMEM((8, 272, 128), jnp.int16),
            pltpu.VMEM((2, 2, 2, 272, 128), jnp.int16),
            pltpu.VMEM((4, 272, 128), jnp.int16),
            pltpu.VMEM((4, 272, 128), jnp.int16),
            pltpu.VMEM((256, 128), F32),
            pltpu.VMEM((4, 2, 272, 128), jnp.int16),
            dma((3,)), one, one, one, one, dma((4,)), dma((3,)),
            one, one, one, dma((8, NCH)), dma((8, NCH)), one, dma((3,)),
            one, one, one, dma((2,)), one, one, pltpu.SemaphoreType.REGULAR((3,)),
            one, one,
        ],
        compiler_params=pltpu.CompilerParams(
            collective_id=0, has_side_effects=True, vmem_limit_bytes=54976 * 1024
        ),
        cost_estimate=pl.CostEstimate(flops=1200000000, bytes_accessed=400000, transcendentals=0),
    )(snapshots, node_owner.reshape(1, ND), mass_blocks.reshape(16, 16, 128))


def solution(mesh):
    placed = (P("blk", "rows"), P("rows", None), P("rows", "blk", None, None), P("rows", "blk"))
    return jax.shard_map(
        per_device, mesh=mesh, in_specs=placed, out_specs=P("rows", "blk"), check_vma=False
    )
```

```python
import jax
import jax.numpy as jnp
from jax import lax
from jax.experimental import pallas as pl
from jax.experimental.pallas import tpu as pltpu
from jax.sharding import PartitionSpec as P

MESH = pl.DeviceIdType.MESH
F32 = jnp.float32
BF16 = jnp.bfloat16
NZ = 16
NR = 16
ND = 512
SD = 128
NCH = 4
CH = SD // NCH
FULL = 32767.0
T0 = (((0,), (0,)), ((), ()))
T1 = (((1,), (1,)), ((), ()))


def codes_of(raw, q):
    v = raw[q, 16:32, :].astype(F32)
    own = jnp.concatenate([v[i : i + 1, :] for i in range(4)], axis=1)
    rank = jnp.concatenate([v[i : i + 1, :] for i in range(4, 8)], axis=1)
    return own, rank


def onehot(row, n):
    ids = lax.broadcasted_iota(jnp.int32, (n, row.shape[1]), 0).astype(F32)
    return jnp.where(ids == row, 1.0, 0.0).astype(BF16)


def encode(g, ref, *at):
    top = jnp.clip(jnp.max(jnp.abs(g), axis=0, keepdims=True), 1e-30, 1e30)
    e = jnp.ceil(jnp.log2(top))
    q = jnp.round(g * (FULL * jnp.exp2(-e)))
    ref[(*at, slice(0, 256), slice(None))] = q.astype(jnp.int32).astype(jnp.int16)
    ref[(*at, slice(256, 272), slice(None))] = jnp.broadcast_to(e, (16, 128)).astype(jnp.int32).astype(jnp.int16)


def decode(v):
    e = v[256:272, :].astype(jnp.int32).astype(F32)[0:1, :]
    return v[0:256, :].astype(jnp.int32).astype(F32) * (jnp.exp2(e) * (1.0 / FULL))


def kernel(
    snap, owner, mass, out,
    own_v, mass_v, msg, raw, mz, cbuf, halo, sall, acc, wown, wc, gt, yrecv, xsend, xrecv, xown, drecv,
    i_sem, t_send, t_recv, a_send, a_recv, c_send, c_recv,
    h_send, h_recv, z_send, r_recv, l_recv, s_send, s_recv,
    w_send, w_recv, y_send, y_recv, x_send, x_recv, f_sem, d_send, d_recv,
):
    blk, s = lax.axis_index("blk"), lax.axis_index("rows")
    yl, z = blk // NZ, lax.rem(blk, NZ)
    x, yh, c = s // 4, lax.rem(s // 2, 2), lax.rem(s, 2)
    sib = s + 1 - 2 * c

    def zmove(k):
        return lax.rem(z + k + NZ, NZ)

    def to(src, dst, ssem, rsem, b, r):
        return pltpu.make_async_remote_copy(
            src_ref=src, dst_ref=dst, send_sem=ssem, recv_sem=rsem, device_id=(b, r), device_id_type=MESH
        )

    def drain(ref, sem):
        pltpu.make_async_copy(ref, ref, sem).wait()

    barrier = pltpu.get_barrier_semaphore()
    for k in (2, -2, 1, -1):
        pl.semaphore_signal(barrier, inc=1, device_id=(yl * NZ + zmove(k), s), device_id_type=MESH)
    plane = yl * NR + s

    def greet(i, carry):
        other = lax.rem(plane + i, 2 * NR)
        pl.semaphore_signal(
            barrier, inc=1, device_id=((other // NR) * NZ + z, lax.rem(other, NR)), device_id_type=MESH
        )
        return carry

    lax.fori_loop(1, 2 * NR, greet, 0)

    in_own = pltpu.make_async_copy(owner, own_v, i_sem.at[0])
    in_mass = pltpu.make_async_copy(mass, mass_v, i_sem.at[1])
    in_snap = pltpu.make_async_copy(snap, sall.at[c, z], i_sem.at[2])
    in_own.start()
    in_mass.start()
    in_snap.start()

    before = jnp.where(
        lax.broadcasted_iota(jnp.int32, (ND, ND), 0) < lax.broadcasted_iota(jnp.int32, (ND, ND), 1), 1.0, 0.0
    ).astype(BF16)
    in_own.wait()
    own = own_v[...].astype(F32)
    mine = onehot(own, NR)
    counts = jnp.dot(mine, before, preferred_element_type=F32)
    rank = jnp.sum(mine.astype(F32) * counts, axis=0, keepdims=True)
    row = lax.broadcasted_iota(jnp.int32, (16, 128), 0)
    code = jnp.zeros((16, 128), F32)
    for i in range(4):
        code = jnp.where(row == i, own[:, 128 * i : 128 * i + 128], code)
        code = jnp.where(row == i + 4, rank[:, 128 * i : 128 * i + 128], code)
    code = code.astype(BF16)
    odd = lax.rem(z, 2)
    in_mass.wait()
    for a in range(NR):
        msg[a, 0:16, :] = mass_v[jnp.where(odd == 1, a // 2, a)]
        msg[a, 16:32, :] = code
    raw[s] = msg[s]
    in_snap.wait()

    pl.semaphore_wait(barrier, 2 * NR - 1 + 4)

    def round_signal(n):
        for k in (2, -2, 1, -1) if n == 0 else (2, -2):
            pl.semaphore_signal(f_sem.at[n], inc=1, device_id=(yl * NZ + zmove(k), s), device_id_type=MESH)

    def round_wait(n):
        pl.semaphore_wait(f_sem.at[n], 4 if n == 0 else 2)

    round_signal(0)

    def scatter(i, carry):
        a = lax.rem(s + i, NR)
        to(msg.at[a], raw.at[s], t_send, t_recv, blk, a).start()
        return carry

    lax.fori_loop(1, NR, scatter, 0)

    def ring(k, h, right):
        ref = sall.at[c, zmove(1 - k if right else k - 1), pl.ds(CH * h, CH)]
        rs = r_recv if right else l_recv
        return to(ref, ref, z_send, rs.at[k - 1, h], yl * NZ + zmove(1 if right else -1), s)

    def on_ring(k, h, right):
        return k < 8 or right == (h < NCH // 2)

    def sibling(k):
        for slot in {0: (0,), 8: (8,)}.get(k, (-k, k)):
            ref = sall.at[c, zmove(slot)]
            to(ref, ref, s_send, s_recv.at[max(k // 2 - 2, 0)], blk, sib).start()

    def ring_step(k):
        for h in range(NCH):
            for right in (True, False):
                if on_ring(k, h, right):
                    ref = sall.at[c, zmove(-k if right else k), pl.ds(CH * h, CH)]
                    drain(ref, (r_recv if right else l_recv).at[k - 1, h])
                    if k < 8 and on_ring(k + 1, h, right):
                        ring(k + 1, h, right).start()
        sibling(k)

    for h in range(NCH):
        for right in (True, False):
            ring(1, h, right).start()
    sibling(0)

    def halo_copy(dyl, ds):
        return to(
            sall.at[c, z], halo.at[2 - 2 * ds + yl], h_send, h_recv, lax.rem(yl + dyl, 2) * NZ + z, s + ds
        )

    halo[2 + yl] = sall[c, z]
    round_wait(0)
    round_signal(1)

    useful = jnp.logical_or(odd == 0, lax.rem(s, 2) == 0)
    kind = jnp.where(odd == 1, 0, jnp.where(s < 8, 1, 2))
    part = jnp.where(odd == 1, s // 2, lax.rem(s, 8))
    shift = jnp.where(odd == 1, 1, jnp.where(s < 8, 0, -1))
    col = jnp.clip(yl * 8 + z // 2 + shift, 0, NR - 1)
    round_wait(1)
    round_signal(2)
    ring_step(1)
    drain(raw.at[0:15], t_recv)

    round_wait(2)

    @pl.when(useful)
    def _():
        own_c, rank_c = codes_of(raw, col)
        slices = raw[:, 0:16, :].reshape(256, 128)
        picked = jnp.dot(slices, onehot(rank_c, 128), preferred_element_type=F32)
        kept = jnp.zeros((16, ND), F32)
        for d in range(NR):
            kept = jnp.where(own_c == float(d), picked[16 * d : 16 * d + 16, :], kept)
        mz[z // 4] = kept.astype(BF16)
        for k in (8, 4, -4):
            to(mz.at[z // 4], mz.at[z // 4], a_send, a_recv, yl * NZ + zmove(k), s).start()

    for ds in (0, -1, 1):
        for dyl in (0, 1):
            if ds == 0:
                if dyl == 1:
                    halo_copy(dyl, ds).start()
            else:
                pl.when(jnp.logical_and(s + ds >= 0, s + ds < NR))(
                    lambda dyl=dyl, ds=ds: halo_copy(dyl, ds).start()
                )
    ring_step(2)
    ring_step(3)

    def spread(f):
        def each(m, carry):
            cc = yl * 8 + (lax.rem(z, 4) + 4 * m) // 2 + shift
            pl.when(jnp.logical_and(useful, jnp.logical_and(cc >= 0, cc < NR)))(lambda: f(m, cc))
            return carry

        lax.fori_loop(0, 4, each, 0)

    def spread_start(m, cc):
        dst = cbuf.at[kind, part]
        for k in (2, 1, -1, 0):
            for dyl in (1, 0):
                copy = to(
                    mz.at[m], dst, c_send.at[m], c_recv.at[kind], lax.rem(yl + dyl, 2) * NZ + zmove(k), cc
                )
                if k == 0 and dyl == 0:
                    pl.when(cc != s)(lambda copy=copy: copy.start())
                    pl.when(cc == s)(lambda: pltpu.make_async_copy(mz.at[m], dst, c_recv.at[kind]).start())
                else:
                    copy.start()

    def spread_sent(m, cc):
        pl.when(cc == s)(lambda: drain(cbuf.at[0, 0:7], c_send.at[m]))
        pl.when(cc != s)(lambda: drain(cbuf.at[0], c_send.at[m]))

    pl.when(useful)(lambda: drain(mz.at[0:3], a_recv))
    spread(spread_start)
    ring_step(4)
    ring_step(5)

    acc[...] = jnp.zeros_like(acc)
    own_s, _ = codes_of(raw, s)
    hot_s = onehot(own_s, NR)
    edge = jnp.logical_or(s == 0, s == NR - 1)
    pl.when(edge)(lambda: drain(halo.at[0:3], h_recv))
    pl.when(jnp.logical_not(edge))(lambda: drain(halo.at[0:5], h_recv))

    def weigh(j):
        @pl.when(jnp.logical_and(s - 1 + j >= 0, s - 1 + j < NR))
        def _():
            drain(cbuf.at[j], c_recv.at[j])
            own_j, rank_j = codes_of(raw, s - 1 + j)
            same = lax.dot_general(onehot(own_j, NR), hot_s, T0, preferred_element_type=F32)
            wide = lax.dot_general(onehot(rank_j, 128), cbuf[j].reshape(128, ND), T0, preferred_element_type=F32)
            m = (wide * same).astype(BF16)
            acc[...] += jnp.dot(halo[pl.ds(2 * j, 2)].reshape(2 * SD, ND), m, preferred_element_type=F32)

    weigh(0)
    weigh(1)
    weigh(2)
    wown[...] = acc[...].reshape(2, SD, ND).astype(BF16)
    to(wown.at[1 - c], wc.at[c], w_send, w_recv, blk, sib).start()
    wc[c] = wown[c]
    ring_step(6)
    drain(wc.at[0], w_recv)

    def tile(d):
        u = lax.rem(z // 2 + d + 8, 8)
        pair = pl.ds(2 * u, 2)
        g = lax.dot_general(sall[0, pair].reshape(2 * SD, ND), wc[0], T1, preferred_element_type=F32)
        g += lax.dot_general(sall[1, pair].reshape(2 * SD, ND), wc[1], T1, preferred_element_type=F32)
        encode(g, gt, u)
        if d == 4:
            home, dst, ssem, rsem = (2 * yl + u // 4) * 4 + lax.rem(u, 4), drecv.at[x, yh], d_send, d_recv
        else:
            home, dst, ssem = x * 4 + lax.rem(u, 4), yrecv.at[yl, yh, u // 4], y_send
            rsem = y_recv.at[0 if -2 <= d < 2 else 1]
        far = jnp.logical_or(home != s, c != yl)
        pl.when(far)(lambda: to(gt.at[u], dst, ssem, rsem, c * NZ + z, home).start())
        pl.when(jnp.logical_not(far))(lambda: pltpu.make_async_copy(gt.at[u], dst, rsem).start())

    drain(sall.at[0, 0:11], s_recv.at[0])
    for d in (0, -1, 1, -2, 2):
        tile(d)
    ring_step(7)
    drain(sall.at[0, 0:4], s_recv.at[1])
    tile(-3)
    tile(3)
    first = jnp.where(lax.rem(2 * yh + c - z // 2 + 10, 8) < 4, 0, 1)
    last = lax.rem(z // 2, 4) == 2 * yh + c
    direct = jnp.logical_and(last, lax.rem(x + first, 2) == 1)

    def half(late):
        i = lax.rem(first + late, 2)
        drain(yrecv.at[0, :, 0:2], y_recv.at[late])
        for y in range(2):
            dest = 2 * y + i
            total = decode(yrecv[y, 0, i]) + decode(yrecv[y, 1, i])

            @pl.when(x == dest)
            def _():
                xown[...] = total

            @pl.when(x != dest)
            def _():
                encode(total, xsend, dest)
                to(xsend.at[dest], xrecv.at[x], x_send, x_recv, blk, 4 * dest + 2 * yh + c).start()

    ring_step(8)
    half(0)
    drain(sall.at[0, 0:1], s_recv.at[2])
    tile(4)

    pl.when(jnp.logical_not(last))(lambda: half(1))

    @pl.when(direct)
    def _():
        drain(drecv, d_recv)
        total = decode(drecv[0, 0]) + decode(drecv[0, 1])
        for k in range(1, 4):
            total += decode(drecv[k, 0]) + decode(drecv[k, 1])
        out[...] = total

    @pl.when(jnp.logical_not(direct))
    def _():
        drain(xrecv.at[0:3], x_recv)
        total = xown[...]
        for k in range(1, 4):
            total += decode(xrecv[lax.rem(x + k, 4)])
        out[...] = total

    drain(msg.at[0:15], t_send)
    pl.when(useful)(lambda: drain(mz.at[0:3], a_send))
    spread(spread_sent)
    pl.when(edge)(lambda: drain(halo.at[0:3], h_send))
    pl.when(jnp.logical_not(edge))(lambda: drain(halo.at[0:5], h_send))
    drain(sall.at[0, 0:15], z_send)
    drain(sall.at[0], s_send)
    drain(wc.at[0], w_send)
    own_y = c == yl
    pl.when(jnp.logical_not(own_y))(lambda: drain(gt.at[0:7], y_send))
    pl.when(jnp.logical_and(own_y, last))(lambda: drain(gt.at[0:6], y_send))
    pl.when(jnp.logical_and(own_y, jnp.logical_not(last)))(lambda: drain(gt.at[0:5], y_send))
    u_last = lax.rem(z // 2 + 4, 8)
    self_last = jnp.logical_and(own_y, (2 * yl + u_last // 4) * 4 + lax.rem(u_last, 4) == s)
    pl.when(jnp.logical_not(self_last))(lambda: drain(gt.at[0], d_send))
    pl.when(jnp.logical_not(last))(lambda: drain(xsend.at[0:3], x_send))
    pl.when(direct)(lambda: drain(xsend.at[0:2], x_send))
    pl.when(jnp.logical_and(last, jnp.logical_not(direct)))(lambda: drain(xsend.at[0], x_send))


def per_device(snapshots, node_owner, mass_blocks, mass_cols):
    dma = pltpu.SemaphoreType.DMA
    one = dma(())
    return pl.pallas_call(
        kernel,
        out_shape=jax.ShapeDtypeStruct((256, 128), F32),
        in_specs=[pl.BlockSpec(memory_space=pl.ANY)] * 3,
        out_specs=pl.BlockSpec(memory_space=pltpu.VMEM),
        scratch_shapes=[
            pltpu.VMEM((1, ND), jnp.int32),
            pltpu.VMEM((16, 16, 128), BF16),
            pltpu.VMEM((16, 32, 128), BF16),
            pltpu.VMEM((16, 32, 128), BF16),
            pltpu.VMEM((4, 16, ND), BF16),
            pltpu.VMEM((3, 8, 16, ND), BF16),
            pltpu.VMEM((6, SD, ND), BF16),
            pltpu.VMEM((2, NZ, SD, ND), BF16),
            pltpu.VMEM((2 * SD, ND), F32),
            pltpu.VMEM((2, SD, ND), BF16),
            pltpu.VMEM((2, SD, ND), BF16),
            pltpu.VMEM((8, 272, 128), jnp.int16),
            pltpu.VMEM((2, 2, 2, 272, 128), jnp.int16),
            pltpu.VMEM((4, 272, 128), jnp.int16),
            pltpu.VMEM((4, 272, 128), jnp.int16),
            pltpu.VMEM((256, 128), F32),
            pltpu.VMEM((4, 2, 272, 128), jnp.int16),
            dma((3,)), one, one, one, one, dma((4,)), dma((3,)),
            one, one, one, dma((8, NCH)), dma((8, NCH)), one, dma((3,)),
            one, one, one, dma((2,)), one, one, pltpu.SemaphoreType.REGULAR((3,)),
            one, one,
        ],
        compiler_params=pltpu.CompilerParams(
            collective_id=0, has_side_effects=True, vmem_limit_bytes=54976 * 1024
        ),
        cost_estimate=pl.CostEstimate(flops=1200000000, bytes_accessed=400000, transcendentals=0),
    )(snapshots, node_owner.reshape(1, ND), mass_blocks.reshape(16, 16, 128))


def solution(mesh):
    placed = (P("blk", "rows"), P("rows", None), P("rows", "blk", None, None), P("rows", "blk"))
    return jax.shard_map(
        per_device, mesh=mesh, in_specs=placed, out_specs=P("rows", "blk"), check_vma=False
    )
```
